256 devices in a mesh: dp: 8 (over z_hi, core), seq: 32 (over z_lo, y, x).
Axes of the slice: x: 4, y: 4, z: 8 (z_hi: 4, z_lo: 2; z = z_hi * 2 + z_lo), core: 2. Of those that a mesh axis runs over, the one named last changes fastest.
Arguments:
- tokens: bfloat16 [8, 64, 64, 1152], P('dp', 'seq'), may hold values from -24 to 24
- cotangent: bfloat16 [8, 64, 64, 1152], P('dp', 'seq'), may hold values from -6 to 6
- w_qkv: bfloat16 [1152, 1728], replicated, may hold values from -5 to 5
- w_out: bfloat16 [576, 1152], replicated, may hold values from -0.25 to 0.25
Outputs:
- result: bfloat16 [8, 64, 64, 1152], P('dp', 'seq')
- grad_tokens: bfloat16 [8, 64, 64, 1152], P('dp', 'seq')
- grad_w_qkv: float32 [1152, 1728], P('seq', 'dp')
- grad_w_out: float32 [576, 1152], P('seq', 'dp')
The draws below stay inside these ranges and needn't reach their ends.
All inputs are finite; a program needn't handle non-finite values.
Results may differ from the reference program's by a relative error of at most 0.034.
Values may be sent and summed in bfloat16 or wider, within the bound.
A program may use at most 64 MiB of HBM per device.

```python
import jax
import jax.numpy as jnp
from jax import lax

D = 1152
HEADS = 8
HS = 72
POS = 64
HD = 576
FRAMES = 64
CLIPS = 8


def draw_tokens(key, part):
    key = jax.random.fold_in(key, 11)
    second = jax.random.fold_in(key, 1)
    shape = (CLIPS, FRAMES, POS, D)
    values = jnp.clip(jax.random.normal(second, shape, jnp.float32), -6.0, 6.0)
    return values.astype(jnp.bfloat16)


def draw_w_qkv(key, part):
    key = jax.random.fold_in(key, 23)
    first = jax.random.fold_in(key, 0)
    base = jnp.clip(jax.random.normal(first, (D, 3 * HD), jnp.float32), -5.0, 5.0) * D ** (-0.5)
    values = base
    return values.astype(jnp.bfloat16)


def level_of(rng, shape, pieces, least, top_value):
    gain = 1.0
    for dim, parts in pieces:
        draws = jax.random.uniform(jax.random.fold_in(jax.random.fold_in(rng, 6), dim), (parts,), jnp.float32, least / len(pieces), top_value / len(pieces))
        gain = gain * jnp.repeat(jnp.exp(draws), shape[dim] // parts).reshape((-1,) + (1,) * (len(shape) - 1 - dim))
    return gain


def scatter_about(rng, dims, width, most, cuts=(), dtype=jnp.bfloat16):
    entries = jax.random.normal(rng, dims, jnp.float32) * width
    if len(cuts) > 0:
        entries = level_of(rng, dims, cuts, -0.22, 0.18) * entries
    return jnp.clip(entries, min=-most, max=most).astype(dtype)


def setup_inputs(seed: int = 0) -> dict:
    key_list = jax.random.split(jax.random.key(seed), 5)
    return {
        "tokens": draw_tokens(jax.random.fold_in(key_list[4], 71), 0),
        "cotangent": scatter_about(key_list[1], (CLIPS, FRAMES, POS, D), 1.0, 6.0, ((0, 8), (1, 32))),
        "w_qkv": draw_w_qkv(jax.random.fold_in(key_list[4], 71), 0),
        "w_out": scatter_about(key_list[3], (HD, D), HD ** -0.5, 0.25),
    }


epsilon = 1e-06

def normalize(values):
    widened = values.astype(jnp.float32)
    centered = widened - lax.optimization_barrier(jnp.mean(widened, axis=-1, keepdims=True))
    inv_std = lax.rsqrt(lax.optimization_barrier(jnp.mean(centered * centered, axis=-1, keepdims=True)) + epsilon)
    return (centered * inv_std, inv_std)

def clip_block(clip_tokens, clip_grad, w_qkv, w_out):
    softmax_scale = HS ** (-0.5)
    rows_total = FRAMES * POS
    x_hat, inv_std = normalize(clip_tokens)
    flat_normed = x_hat.astype(jnp.bfloat16).reshape(rows_total, D)
    projected = jnp.dot(flat_normed, w_qkv, preferred_element_type=jnp.float32).astype(jnp.bfloat16)
    projected = projected.reshape(FRAMES, POS, 3, HEADS, HS).astype(jnp.float32)
    query_rows = projected[:, :, 0]
    key_rows = projected[:, :, 1]
    value_rows = projected[:, :, 2]
    scores = jnp.einsum('fphe,gphe->phfg', query_rows, key_rows) * softmax_scale
    top = lax.optimization_barrier(jnp.max(scores, axis=-1, keepdims=True))
    expo = jnp.exp(scores - top)
    probs = expo / lax.optimization_barrier(jnp.sum(expo, axis=-1, keepdims=True))
    probs_low = probs.astype(jnp.bfloat16).astype(jnp.float32)
    attended = jnp.einsum('phfg,gphe->fphe', probs_low, value_rows).astype(jnp.bfloat16)
    flat_out = attended.reshape(rows_total, HD)
    branch = jnp.dot(flat_out, w_out, preferred_element_type=jnp.float32)
    result = (clip_tokens.astype(jnp.float32) + branch.reshape(FRAMES, POS, D)).astype(jnp.bfloat16)
    flat_grad = clip_grad.reshape(rows_total, D)
    grad_attended = jnp.dot(flat_grad, w_out.T, preferred_element_type=jnp.float32).astype(jnp.bfloat16)
    grad_w_out = jnp.dot(flat_out.T, flat_grad, preferred_element_type=jnp.float32)
    grad_heads = grad_attended.reshape(FRAMES, POS, HEADS, HS).astype(jnp.float32)
    grad_probs = jnp.einsum('fphe,gphe->phfg', grad_heads, value_rows)
    delta = lax.optimization_barrier(jnp.sum(probs * grad_probs, axis=-1, keepdims=True))
    grad_scores = (probs * (grad_probs - delta) * softmax_scale).astype(jnp.bfloat16).astype(jnp.float32)
    grad_query = jnp.einsum('phfg,gphe->fphe', grad_scores, key_rows).astype(jnp.bfloat16)
    grad_key = jnp.einsum('phfg,fphe->gphe', grad_scores, query_rows).astype(jnp.bfloat16)
    grad_value = jnp.einsum('phfg,fphe->gphe', probs_low, grad_heads).astype(jnp.bfloat16)
    grad_proj = jnp.stack([grad_query, grad_key, grad_value], axis=2).reshape(rows_total, 3 * HD)
    grad_w_qkv = jnp.dot(flat_normed.T, grad_proj, preferred_element_type=jnp.float32)
    grad_normed = jnp.dot(grad_proj, w_qkv.T, preferred_element_type=jnp.float32).reshape(FRAMES, POS, D)
    first = lax.optimization_barrier(jnp.mean(grad_normed, axis=-1, keepdims=True))
    second = lax.optimization_barrier(jnp.mean(grad_normed * x_hat, axis=-1, keepdims=True))
    grad_branch = ((grad_normed - first - x_hat * second) * inv_std).astype(jnp.bfloat16)
    grad_branch = lax.optimization_barrier(grad_branch)
    grad_tokens = (clip_grad.astype(jnp.float32) + grad_branch.astype(jnp.float32)).astype(jnp.bfloat16)
    return (result, grad_tokens, grad_w_qkv, grad_w_out)

def reference(tokens, cotangent, w_qkv, w_out):

    def step(carry, pair):
        result, grad_tokens, grad_w_qkv, grad_w_out = clip_block(pair[0], pair[1], w_qkv, w_out)
        return ((carry[0] + grad_w_qkv, carry[1] + grad_w_out), (result, grad_tokens))
    start = (jnp.zeros((D, 3 * HD), jnp.float32), jnp.zeros((HD, D), jnp.float32))
    sums, outputs = lax.scan(step, start, (tokens, cotangent))
    factor = (CLIPS * FRAMES * POS) ** (-0.5)
    return (outputs[0], outputs[1], sums[0] * factor, sums[1] * factor)
```

```python
import functools

import jax
import jax.numpy as jnp
from jax import lax
from jax.experimental import pallas as pl
from jax.experimental.pallas import tpu as pltpu
from jax.sharding import PartitionSpec as P

MESH = pl.DeviceIdType.MESH
F32, BF16 = jnp.float32, jnp.bfloat16

D = 1152
HEADS = 8
HS = 72
HD = 576
ROWS = 128
SEQ = 32
PLANE = 16
EPS = 1e-6
SCALE = HS ** (-0.5)
FACTOR = 32768 ** (-0.5)


def dot(a, b, contract):
    return lax.dot_general(a, b, ((contract[:1], contract[1:]), ((), ())), preferred_element_type=F32)


def kernel(
    tok, cot, wqkv_hbm, wout_hbm,
    result, gtok, gwq, gwo,
    wqkv, wout,
    wide, slim, xhat, cotp,
    xs, xr, gs, gr, ats, atr, gbs, gbr,
    cotq, cotr, ntr, arr, amine, apart, gph, gpart, tmine, tpart,
    qb, kb, vb, gab, probs, plow,
    dsend, drecv, dsum, zsend, zrecv, wsend, wrecv, wsum, vsend, vrecv,
    wsem, x_ss, x_rs, g_ss, g_rs, at_ss, at_rs, gb_ss, gb_rs, c_ss, c_rs,
    d_ss, d_rs, z_ss, z_rs, w_ss, w_rs, v_ss, v_rs,
):
    dp, seq = lax.axis_index("dp"), lax.axis_index("seq")
    core, z_hi = dp % 2, dp // 2
    xy, z_lo = seq % PLANE, seq // PLANE
    mate = z_hi * 2 + 1 - core
    zed = z_hi * 2 + z_lo

    def remote(src, dst, send_sem, recv_sem, to_dp, to_seq):
        return pltpu.make_async_remote_copy(
            src_ref=src, dst_ref=dst, send_sem=send_sem, recv_sem=recv_sem,
            device_id=(to_dp, to_seq), device_id_type=MESH,
        )

    barrier = pltpu.get_barrier_semaphore()

    def greet(to_dp, to_seq):
        pl.semaphore_signal(barrier, inc=1, device_id=(to_dp, to_seq), device_id_type=MESH)

    @pl.loop(1, SEQ)
    def _(k):
        greet(dp, (seq + k) % SEQ)

    @pl.loop(1, 8)
    def _(k):
        greet((dp + k) % 8, xy)
        greet((dp + k) % 8, PLANE + xy)

    @pl.loop(1, PLANE)
    def _(k):
        greet(mate, z_lo * PLANE + (xy + k) % PLANE)

    load_wqkv = pltpu.make_async_copy(wqkv_hbm, wqkv, wsem.at[0])
    load_wout = pltpu.make_async_copy(wout_hbm, wout, wsem.at[1])
    load_wout.start()
    load_wqkv.start()

    new = lax.broadcasted_iota(jnp.int32, (ROWS, ROWS), 0)
    old = lax.broadcasted_iota(jnp.int32, (ROWS, ROWS), 1)
    place = ((new >> 1) & 1) * 64 + (new >> 2) * 2 + (new & 1)
    move = jnp.where(place == old, 1.0, 0.0).astype(BF16)

    def pack(rows, block):
        for p in range(SEQ):
            block[p] = rows[4 * p : 4 * p + 4, :].astype(BF16)

    def unpack(block, rows):
        for p in range(SEQ):
            rows[4 * p : 4 * p + 4, :] = block[p].astype(F32)

    def push_all(src, dst, ss, rs):
        @pl.loop(1, SEQ)
        def _(k):
            to = (seq + k) % SEQ
            remote(src.at[to], dst.at[seq], ss.at[to], rs.at[seq], dp, to).start()

        dst[seq] = src[seq]

    def take_all(src, dst, ss, rs):
        @pl.loop(1, SEQ)
        def _(k):
            come = (seq + k) % SEQ
            remote(src.at[come], dst.at[come], ss.at[come], rs.at[come], dp, come).wait_recv()

    def sent_all(src, dst, ss, rs):
        @pl.loop(1, SEQ)
        def _(k):
            to = (seq + k) % SEQ
            remote(src.at[to], dst.at[to], ss.at[to], rs.at[to], dp, to).wait_send()

    wide[...] = dot(move, tok[...], (1, 0))
    pack(wide, xs)
    pl.semaphore_wait(barrier, SEQ - 1 + 14 + PLANE - 1)
    push_all(xs, xr, x_ss, x_rs)

    cotp[...] = dot(move, cot[...], (1, 0)).astype(BF16)
    load_wout.wait()
    slim[...] = dot(cotp[...], wout[...], (1, 1))
    pack(slim, gs)
    push_all(gs, gr, g_ss, g_rs)
    for q in range(4):
        cotq[q] = cotp[:, 288 * q : 288 * q + 288]
    swap_cot = remote(cotq.at[pl.ds(2 * (1 - core), 2)], cotr, c_ss.at[0], c_rs.at[0], mate, seq)
    swap_cot.start()

    take_all(xs, xr, x_ss, x_rs)
    unpack(xr, wide)
    x = wide[...]
    centered = x - jnp.mean(x, axis=-1, keepdims=True)
    inv_std = lax.rsqrt(jnp.mean(centered * centered, axis=-1, keepdims=True) + EPS)
    x_hat = centered * inv_std
    xhat[...] = x_hat
    load_wqkv.wait()
    projected = dot(x_hat.astype(BF16), wqkv[...], (1, 0))
    query = projected[:, :HD].astype(BF16)
    key = projected[:, HD : 2 * HD].astype(BF16)
    value = projected[:, 2 * HD :].astype(BF16)
    lane = lax.broadcasted_iota(jnp.int32, (ROWS, HD), 1)

    def stack(block, out):
        wide_block = block.astype(F32)
        for h in range(HEADS):
            inside = (lane >= h * HS) & (lane < (h + 1) * HS)
            out[h * ROWS : (h + 1) * ROWS, :] = jnp.where(inside, wide_block, 0.0).astype(BF16)

    def side(block):
        return jnp.concatenate([block[h * ROWS : (h + 1) * ROWS, :] for h in range(HEADS)], axis=1)

    stack(query, qb)
    stack(value, vb)
    scores = dot(qb[...], key, (1, 1)) * SCALE
    here = lax.broadcasted_iota(jnp.int32, (HEADS * ROWS, ROWS), 0)
    there = lax.broadcasted_iota(jnp.int32, (HEADS * ROWS, ROWS), 1)
    scores = jnp.where(((here ^ there) & 1) == 0, scores, -jnp.inf)
    expo = jnp.exp(scores - jnp.max(scores, axis=-1, keepdims=True))
    prob = expo / jnp.sum(expo, axis=-1, keepdims=True)
    probs[...] = prob
    plow[...] = prob.astype(BF16)
    slim[...] = dot(side(plow), vb[...], (1, 0))
    pack(slim, ats)
    push_all(ats, atr, at_ss, at_rs)

    ntr[...] = xhat[...].T
    for p in range(PLANE):
        arr[80 * p : 80 * p + 36, :] = ntr[36 * p : 36 * p + 36, :]
        arr[80 * p + 36 : 80 * p + 72, :] = ntr[36 * (PLANE + p) : 36 * (PLANE + p) + 36, :]
        arr[80 * p + 72 : 80 * p + 80, :] = jnp.zeros((8, ROWS), F32)
    amine[...] = arr[...].astype(BF16)
    swap_a = remote(amine, apart, c_ss.at[1], c_rs.at[1], mate, seq)
    swap_a.start()

    stack(key, kb)
    take_all(gs, gr, g_ss, g_rs)
    unpack(gr, slim)
    stack(slim[...], gab)
    grad_probs = dot(gab[...], value, (1, 1))
    prob = probs[...]
    delta = jnp.sum(prob * grad_probs, axis=-1, keepdims=True)
    grad_scores = (prob * (grad_probs - delta) * SCALE).astype(BF16)
    grad_query = dot(side(grad_scores), kb[...], (1, 0))
    grad_key = dot(grad_scores, qb[...], (0, 0))
    grad_value = dot(plow[...], gab[...], (0, 0))
    grad_proj = jnp.concatenate([grad_query, grad_key, grad_value], axis=1)
    gph[0] = grad_proj[:, :864].astype(BF16)
    gph[1] = grad_proj[:, 864:].astype(BF16)
    swap_g = remote(gph.at[1 - core], gpart, c_ss.at[2], c_rs.at[2], mate, seq)
    swap_g.start()
    grad_proj = grad_proj.astype(BF16)

    swap_a.wait_recv()
    swap_g.wait_recv()
    right = jnp.concatenate([gph[core], gpart[...]], axis=0)

    def plane_copy(k):
        to = (xy + k) % PLANE
        return remote(
            dsend.at[to], drecv.at[xy], d_ss.at[to], d_rs.at[xy], dp, z_lo * PLANE + to
        )

    @pl.loop(1, PLANE + 1)
    def _(k):
        to = (xy + k) % PLANE
        rows = pl.ds(pl.multiple_of(to * 80, 16), 80)
        left = jnp.concatenate([amine[rows, :], apart[rows, :]], axis=1)
        dsend[to] = dot(left, right, (1, 0)).astype(BF16)

        @pl.when(k < PLANE)
        def _():
            plane_copy(k).start()

    grad_normed = dot(grad_proj, wqkv[...], (1, 1))
    x_hat = xhat[...]
    first = jnp.mean(grad_normed, axis=-1, keepdims=True)
    second = jnp.mean(grad_normed * x_hat, axis=-1, keepdims=True)
    wide[...] = (grad_normed - first - x_hat * second) * inv_std
    pack(wide, gbs)
    push_all(gbs, gbr, gb_ss, gb_rs)

    take_all(ats, atr, at_ss, at_rs)
    unpack(atr, slim)
    back = slim[...].astype(BF16)
    tmine[...] = slim[...].T.astype(BF16)
    swap_t = remote(tmine, tpart, c_ss.at[3], c_rs.at[3], mate, seq)
    swap_t.start()
    ordered = dot(move, back, (0, 0)).astype(BF16)
    branch = dot(ordered, wout[...], (1, 0))
    result[...] = (tok[...].astype(F32) + branch).astype(BF16)
    swap_cot.wait_recv()
    swap_t.wait_recv()

    def z_target(n):
        return 4 * core + n // 2, (n % 2) * PLANE + xy

    for j in range(2):
        right = jnp.concatenate([cotq[2 * core + j], cotr[j]], axis=0)
        left = jnp.concatenate([tmine[...], tpart[...]], axis=1)
        product = dot(left, right, (1, 0))
        for c in range(2):
            for half in range(2):
                n = (2 * j + c) * 2 + half
                begin = half * 288 + c * 144
                wsend[n] = product[begin : begin + 144, :].astype(BF16)

    def z_push(src, dst, ss, rs):
        @pl.loop(0, 8)
        def _(n):
            to_dp, to_seq = z_target(n)
            own = (to_dp == dp) & (to_seq == seq)

            @pl.when(own)
            def _():
                dst[zed] = src[n]

            @pl.when(jnp.logical_not(own))
            def _():
                remote(src.at[n], dst.at[zed], ss.at[n], rs.at[zed], to_dp, to_seq).start()

    def z_take(src, dst, ss, rs):
        @pl.loop(0, 8)
        def _(n):
            from_dp, from_seq = (n // 2) * 2 + dp // 4, (n % 2) * PLANE + xy

            @pl.when(jnp.logical_not((from_dp == dp) & (from_seq == seq)))
            def _():
                remote(src.at[n], dst.at[n], ss.at[n], rs.at[n], from_dp, from_seq).wait_recv()

    def z_sent(src, dst, ss, rs):
        @pl.loop(0, 8)
        def _(n):
            to_dp, to_seq = z_target(n)

            @pl.when(jnp.logical_not((to_dp == dp) & (to_seq == seq)))
            def _():
                remote(src.at[n], dst.at[n], ss.at[n], rs.at[n], to_dp, to_seq).wait_send()

    z_push(wsend, wrecv, w_ss, w_rs)

    z_take(wsend, wrecv, w_ss, w_rs)
    total = wrecv[0].astype(F32)
    for n in range(1, 8):
        total = total + wrecv[n].astype(F32)
    wsum[0:144, :] = total
    wsum[144:160, :] = jnp.zeros((16, 288), F32)
    for n in range(16):
        begin = (n // 2) * 18
        vsend[n] = wsum[begin : begin + 32, 144 * (n % 2) : 144 * (n % 2) + 144].astype(BF16)

    def v_target(n):
        return z_hi * 2 + n % 2, z_lo * PLANE + 8 * core + n // 2

    @pl.loop(0, 16)
    def _(n):
        to_dp, to_seq = v_target(n)
        own = (to_dp == dp) & (to_seq == seq)

        @pl.when(own)
        def _():
            vrecv[xy] = vsend[n]

        @pl.when(jnp.logical_not(own))
        def _():
            remote(vsend.at[n], vrecv.at[xy], v_ss.at[n], v_rs.at[xy], to_dp, to_seq).start()

    dsum[0:80, :] = dsend[xy].astype(F32)
    dsum[80:96, :] = jnp.zeros((16, 864), F32)

    @pl.loop(1, PLANE)
    def _(k):
        come = (xy + PLANE - k) % PLANE
        remote(
            dsend.at[come], drecv.at[come], d_ss.at[come], d_rs.at[come], dp, z_lo * PLANE + come
        ).wait_recv()
        dsum[0:80, :] += drecv[come].astype(F32)

    for n in range(8):
        begin, column = 36 * (n % 2), 216 * (n // 2)
        zsend[n] = dsum[begin : begin + 48, column : column + 216].astype(BF16)
    z_push(zsend, zrecv, z_ss, z_rs)

    take_all(gbs, gbr, gb_ss, gb_rs)
    unpack(gbr, wide)
    ordered = dot(move, wide[...].astype(BF16), (0, 0))
    gtok[...] = (cot[...].astype(F32) + ordered).astype(BF16)

    @pl.loop(0, 16)
    def _(n):
        from_dp, from_seq = z_hi * 2 + xy // 8, z_lo * PLANE + n

        @pl.when(jnp.logical_not((from_dp == dp) & (from_seq == seq)))
        def _():
            remote(vsend.at[n], vrecv.at[n], v_ss.at[n], v_rs.at[n], from_dp, from_seq).wait_recv()

    total = vrecv[0].astype(F32)
    for n in range(1, 16):
        total = total + vrecv[n].astype(F32)
    gwo[...] = total[:18, :] * FACTOR

    z_take(zsend, zrecv, z_ss, z_rs)
    total = zrecv[0].astype(F32)
    for n in range(1, 8):
        total = total + zrecv[n].astype(F32)
    gwq[...] = total[:36, :] * FACTOR

    sent_all(xs, xr, x_ss, x_rs)
    sent_all(gs, gr, g_ss, g_rs)
    sent_all(ats, atr, at_ss, at_rs)
    sent_all(gbs, gbr, gb_ss, gb_rs)
    swap_cot.wait_send()
    swap_a.wait_send()
    swap_g.wait_send()
    swap_t.wait_send()

    @pl.loop(1, PLANE)
    def _(k):
        plane_copy(k).wait_send()

    z_sent(wsend, wrecv, w_ss, w_rs)
    z_sent(zsend, zrecv, z_ss, z_rs)

    @pl.loop(0, 16)
    def _(n):
        to_dp, to_seq = v_target(n)

        @pl.when(jnp.logical_not((to_dp == dp) & (to_seq == seq)))
        def _():
            remote(vsend.at[n], vrecv.at[n], v_ss.at[n], v_rs.at[n], to_dp, to_seq).wait_send()


def shards(tokens, cotangent, w_qkv, w_out):
    shape = tokens.shape
    vmem = pl.BlockSpec(memory_space=pltpu.VMEM)
    hbm = pl.BlockSpec(memory_space=pl.ANY)
    dma = pltpu.SemaphoreType.DMA
    scratch = [
        ((D, 3 * HD), BF16), ((HD, D), BF16),
        ((ROWS, D), F32), ((ROWS, HD), F32), ((ROWS, D), F32), ((ROWS, D), BF16),
        ((SEQ, 4, D), BF16), ((SEQ, 4, D), BF16), ((SEQ, 4, HD), BF16), ((SEQ, 4, HD), BF16),
        ((SEQ, 4, HD), BF16), ((SEQ, 4, HD), BF16), ((SEQ, 4, D), BF16), ((SEQ, 4, D), BF16),
        ((4, ROWS, 288), BF16), ((2, ROWS, 288), BF16),
        ((D, ROWS), F32), ((80 * PLANE, ROWS), F32),
        ((80 * PLANE, ROWS), BF16), ((80 * PLANE, ROWS), BF16),
        ((2, ROWS, 864), BF16), ((ROWS, 864), BF16), ((HD, ROWS), BF16), ((HD, ROWS), BF16),
        ((HEADS * ROWS, HD), BF16), ((HEADS * ROWS, HD), BF16),
        ((HEADS * ROWS, HD), BF16), ((HEADS * ROWS, HD), BF16),
        ((HEADS * ROWS, ROWS), F32), ((HEADS * ROWS, ROWS), BF16),
        ((PLANE, 80, 864), BF16), ((PLANE, 80, 864), BF16), ((96, 864), F32),
        ((8, 48, 216), BF16), ((8, 48, 216), BF16),
        ((8, 144, 288), BF16), ((8, 144, 288), BF16), ((160, 288), F32),
        ((16, 32, 144), BF16), ((16, 32, 144), BF16),
    ]
    sems = [2] + [SEQ] * 8 + [4, 4, PLANE, PLANE, 8, 8, 8, 8, 16, 16]
    result, gtok, gwq, gwo = pl.pallas_call(
        kernel,
        out_shape=(
            jax.ShapeDtypeStruct((ROWS, D), BF16),
            jax.ShapeDtypeStruct((ROWS, D), BF16),
            jax.ShapeDtypeStruct((36, 216), F32),
            jax.ShapeDtypeStruct((18, 144), F32),
        ),
        in_specs=[vmem, vmem, hbm, hbm],
        out_specs=(vmem,) * 4,
        scratch_shapes=[pltpu.VMEM(s, t) for s, t in scratch] + [dma((n,)) for n in sems],
        compiler_params=pltpu.CompilerParams(
            collective_id=0, has_side_effects=True, vmem_limit_bytes=56 * 1024 * 1024
        ),
    )(tokens.reshape(ROWS, D), cotangent.reshape(ROWS, D), w_qkv, w_out)
    return (result.reshape(shape), gtok.reshape(shape), gwq, gwo)


def solution(mesh):
    in_specs = (P("dp", "seq", None, None), P("dp", "seq", None, None), P(), P())
    out_specs = (
        P("dp", "seq", None, None),
        P("dp", "seq", None, None),
        P("seq", "dp"),
        P("seq", "dp"),
    )
    return jax.shard_map(shards, mesh=mesh, in_specs=in_specs, out_specs=out_specs, check_vma=False)
```

```python
import functools

import jax
import jax.numpy as jnp
from jax import lax
from jax.experimental import pallas as pl
from jax.experimental.pallas import tpu as pltpu
from jax.sharding import PartitionSpec as P

MESH = pl.DeviceIdType.MESH
F32, BF16 = jnp.float32, jnp.bfloat16

D = 1152
HEADS = 8
HS = 72
HD = 576
ROWS = 128
SEQ = 32
PLANE = 16
EPS = 1e-6
SCALE = HS ** (-0.5)
FACTOR = 32768 ** (-0.5)


def dot(a, b, contract):
    return lax.dot_general(a, b, ((contract[:1], contract[1:]), ((), ())), preferred_element_type=F32)


def kernel(
    tok, cot, wqkv_hbm, wout_hbm,
    result, gtok, gwq, gwo,
    wqkv, wout,
    wide, slim, xhat, cotp,
    xs, xr, gs, gr, ats, atr, gbs, gbr,
    cotq, cotr, ntr, arr, amine, apart, gph, gpart, tmine, tpart,
    qb, kb, vb, gab, probs, plow,
    fsend, frelay, fback, own, hsend, hrecv, zsend, zrecv, wsend, wrecv, wsum, vsend, vrecv,
    wsem, x_ss, x_rs, g_ss, g_rs, at_ss, at_rs, gb_ss, gb_rs, c_ss, c_rs,
    f_ss, f_rs, h_ss, h_rs, z_ss, z_rs, w_ss, w_rs, v_ss, v_rs,
):
    dp, seq = lax.axis_index("dp"), lax.axis_index("seq")
    core, z_hi = dp % 2, dp // 2
    xy, z_lo = seq % PLANE, seq // PLANE
    mate = z_hi * 2 + 1 - core
    zed = z_hi * 2 + z_lo
    x, y = xy % 4, xy // 4
    step = 1 + 2 * core

    def remote(src, dst, send_sem, recv_sem, to_dp, to_seq):
        return pltpu.make_async_remote_copy(
            src_ref=src, dst_ref=dst, send_sem=send_sem, recv_sem=recv_sem,
            device_id=(to_dp, to_seq), device_id_type=MESH,
        )

    barrier = pltpu.get_barrier_semaphore()

    def greet(to_dp, to_seq):
        pl.semaphore_signal(barrier, inc=1, device_id=(to_dp, to_seq), device_id_type=MESH)

    @pl.loop(1, SEQ)
    def _(k):
        greet(dp, (seq + k) % SEQ)

    @pl.loop(1, 8)
    def _(k):
        greet((dp + k) % 8, xy)
        greet((dp + k) % 8, PLANE + xy)

    @pl.loop(1, PLANE)
    def _(k):
        greet(mate, z_lo * PLANE + (xy + k) % PLANE)

    load_wqkv = pltpu.make_async_copy(wqkv_hbm, wqkv, wsem.at[0])
    load_wout = pltpu.make_async_copy(wout_hbm, wout, wsem.at[1])
    load_wout.start()
    load_wqkv.start()

    new = lax.broadcasted_iota(jnp.int32, (ROWS, ROWS), 0)
    old = lax.broadcasted_iota(jnp.int32, (ROWS, ROWS), 1)
    place = ((new >> 1) & 1) * 64 + (new >> 2) * 2 + (new & 1)
    move = jnp.where(place == old, 1.0, 0.0).astype(BF16)

    def pack(rows, block):
        for p in range(SEQ):
            block[p] = rows[4 * p : 4 * p + 4, :].astype(BF16)

    def unpack(block, rows):
        for p in range(SEQ):
            rows[4 * p : 4 * p + 4, :] = block[p].astype(F32)

    def push_all(src, dst, ss, rs):
        @pl.loop(1, SEQ)
        def _(k):
            to = (seq + k) % SEQ
            remote(src.at[to], dst.at[seq], ss.at[to], rs.at[seq], dp, to).start()

        dst[seq] = src[seq]

    def take_all(src, dst, ss, rs):
        @pl.loop(1, SEQ)
        def _(k):
            come = (seq + k) % SEQ
            remote(src.at[come], dst.at[come], ss.at[come], rs.at[come], dp, come).wait_recv()

    def sent_all(src, dst, ss, rs):
        @pl.loop(1, SEQ)
        def _(k):
            to = (seq + k) % SEQ
            remote(src.at[to], dst.at[to], ss.at[to], rs.at[to], dp, to).wait_send()

    wide[...] = dot(move, tok[...], (1, 0))
    pack(wide, xs)
    pl.semaphore_wait(barrier, SEQ - 1 + 14 + PLANE - 1)
    push_all(xs, xr, x_ss, x_rs)

    cotp[...] = dot(move, cot[...], (1, 0)).astype(BF16)
    load_wout.wait()
    slim[...] = dot(cotp[...], wout[...], (1, 1))
    pack(slim, gs)
    push_all(gs, gr, g_ss, g_rs)
    for q in range(4):
        cotq[q] = cotp[:, 288 * q : 288 * q + 288]
    swap_cot = remote(cotq.at[pl.ds(2 * (1 - core), 2)], cotr, c_ss.at[0], c_rs.at[0], mate, seq)
    swap_cot.start()

    take_all(xs, xr, x_ss, x_rs)
    unpack(xr, wide)
    moved = wide[...]
    centered = moved - jnp.mean(moved, axis=-1, keepdims=True)
    inv_std = lax.rsqrt(jnp.mean(centered * centered, axis=-1, keepdims=True) + EPS)
    x_hat = centered * inv_std
    xhat[...] = x_hat
    load_wqkv.wait()
    normed = x_hat.astype(BF16)
    query = dot(normed, wqkv[0:HD, :], (1, 1)).astype(BF16)
    key = dot(normed, wqkv[HD : 2 * HD, :], (1, 1)).astype(BF16)
    value = dot(normed, wqkv[2 * HD : 3 * HD, :], (1, 1)).astype(BF16)
    lane = lax.broadcasted_iota(jnp.int32, (ROWS, HD), 1)

    def stack(block, out):
        wide_block = block.astype(F32)
        for h in range(HEADS):
            inside = (lane >= h * HS) & (lane < (h + 1) * HS)
            out[h * ROWS : (h + 1) * ROWS, :] = jnp.where(inside, wide_block, 0.0).astype(BF16)

    def side(block):
        return jnp.concatenate([block[h * ROWS : (h + 1) * ROWS, :] for h in range(HEADS)], axis=1)

    stack(query, qb)
    stack(value, vb)
    scores = dot(qb[...], key, (1, 1)) * SCALE
    here = lax.broadcasted_iota(jnp.int32, (HEADS * ROWS, ROWS), 0)
    there = lax.broadcasted_iota(jnp.int32, (HEADS * ROWS, ROWS), 1)
    scores = jnp.where(((here ^ there) & 1) == 0, scores, -jnp.inf)
    expo = jnp.exp(scores - jnp.max(scores, axis=-1, keepdims=True))
    prob = expo / jnp.sum(expo, axis=-1, keepdims=True)
    probs[...] = prob
    plow[...] = prob.astype(BF16)
    slim[...] = dot(side(plow), vb[...], (1, 0))
    pack(slim, ats)
    push_all(ats, atr, at_ss, at_rs)

    ntr[...] = xhat[...].T
    for p in range(PLANE):
        begin = 144 * (p % 4) + 36 * (p // 4)
        arr[begin : begin + 36, :] = ntr[36 * p : 36 * p + 36, :]
    arr[576:, :] = ntr[576:, :]
    amine[...] = arr[...].astype(BF16)
    swap_a = remote(amine, apart, c_ss.at[1], c_rs.at[1], mate, seq)
    swap_a.start()

    stack(key, kb)
    take_all(gs, gr, g_ss, g_rs)
    unpack(gr, slim)
    stack(slim[...], gab)
    grad_probs = dot(gab[...], value, (1, 1))
    prob = probs[...]
    delta = jnp.sum(prob * grad_probs, axis=-1, keepdims=True)
    grad_scores = (prob * (grad_probs - delta) * SCALE).astype(BF16)
    grad_query = dot(side(grad_scores), kb[...], (1, 0))
    grad_key = dot(grad_scores, qb[...], (0, 0))
    grad_value = dot(plow[...], gab[...], (0, 0))
    grad_proj = jnp.concatenate([grad_query, grad_key, grad_value], axis=1)
    gph[0] = grad_proj[:, :864].astype(BF16)
    gph[1] = grad_proj[:, 864:].astype(BF16)
    swap_g = remote(gph.at[1 - core], gpart, c_ss.at[2], c_rs.at[2], mate, seq)
    swap_g.start()
    grad_proj = grad_proj.astype(BF16)

    take_all(ats, atr, at_ss, at_rs)
    unpack(atr, slim)
    back = slim[...].astype(BF16)
    tmine[...] = slim[...].T.astype(BF16)
    swap_t = remote(tmine, tpart, c_ss.at[3], c_rs.at[3], mate, seq)
    swap_t.start()
    ordered = dot(move, back, (0, 0)).astype(BF16)
    branch = dot(ordered, wout[...], (1, 0))
    result[...] = (tok[...].astype(F32) + branch).astype(BF16)
    swap_a.wait_recv()
    swap_g.wait_recv()
    right_g = jnp.concatenate([gph[core], gpart[...]], axis=0)

    def block(t, to):
        rows = pl.ds(pl.multiple_of(t * 576 + to * 144, 16), 144)
        return dot(jnp.concatenate([amine[rows, :], apart[rows, :]], axis=1), right_g, (1, 0))

    def member(t, r):
        r = r % 4
        return z_lo * PLANE + (4 * y + r if t == 0 else 4 * r + x)

    ring = (x, y)

    def hop(t, n):
        src, dst, ahead = (
            (fsend.at[t, 0, 0:80], frelay.at[t, 0:80], True),
            (fsend.at[t, 0, 80:144], frelay.at[t, 80:144], False),
            (fsend.at[t, 1, 0:80], fback.at[t, 0, 0:80], True),
            (fsend.at[t, 1, 80:144], fback.at[t, 0, 80:144], True),
            (fsend.at[t, 2, 0:80], fback.at[t, 1, 0:80], False),
            (fsend.at[t, 2, 80:144], fback.at[t, 1, 80:144], False),
        )[n]
        to = ring[t] + (step if ahead else 4 - step)
        return remote(src, dst, f_ss.at[t, n], f_rs.at[t, n], dp, member(t, to))

    for t in range(2):
        fsend[t, 0] = block(t, (ring[t] + 2) % 4).astype(BF16)
        hop(t, 0).start()
        hop(t, 1).start()
    swap_cot.wait_recv()
    swap_t.wait_recv()

    def z_target(n):
        return 4 * core + n // 2, (n % 2) * PLANE + xy

    for j in range(2):
        right_c = jnp.concatenate([cotq[2 * core + j], cotr[j]], axis=0)
        left = jnp.concatenate([tmine[...], tpart[...]], axis=1)
        product = dot(left, right_c, (1, 0))
        for c in range(2):
            for half in range(2):
                n = (2 * j + c) * 2 + half
                begin = half * 288 + c * 144
                wsend[n] = product[begin : begin + 144, :].astype(BF16)

    def z_push(src, dst, ss, rs):
        @pl.loop(0, 8)
        def _(n):
            to_dp, to_seq = z_target(n)
            own = (to_dp == dp) & (to_seq == seq)

            @pl.when(own)
            def _():
                dst[zed] = src[n]

            @pl.when(jnp.logical_not(own))
            def _():
                remote(src.at[n], dst.at[zed], ss.at[n], rs.at[zed], to_dp, to_seq).start()

    def z_take(src, dst, ss, rs):
        @pl.loop(0, 8)
        def _(n):
            from_dp, from_seq = (n // 2) * 2 + dp // 4, (n % 2) * PLANE + xy

            @pl.when(jnp.logical_not((from_dp == dp) & (from_seq == seq)))
            def _():
                remote(src.at[n], dst.at[n], ss.at[n], rs.at[n], from_dp, from_seq).wait_recv()

    def z_sent(src, dst, ss, rs):
        @pl.loop(0, 8)
        def _(n):
            to_dp, to_seq = z_target(n)

            @pl.when(jnp.logical_not((to_dp == dp) & (to_seq == seq)))
            def _():
                remote(src.at[n], dst.at[n], ss.at[n], rs.at[n], to_dp, to_seq).wait_send()

    z_push(wsend, wrecv, w_ss, w_rs)

    for t in range(2):
        fsend[t, 1] = block(t, (ring[t] + step) % 4).astype(BF16)
        hop(t, 3).start()
        fsend[t, 2] = block(t, (ring[t] + 4 - step) % 4).astype(BF16)
        hop(t, 4).start()
    for t in range(2):
        own[t, 0:144] = block(t, ring[t])
        own[t, 144:160] = jnp.zeros((16, 864), F32)
    for t in range(2):
        hop(t, 0).wait_recv()
        fsend[t, 1, 0:80] = (fsend[t, 1, 0:80].astype(F32) + frelay[t, 0:80].astype(F32)).astype(BF16)
        hop(t, 2).start()
        hop(t, 1).wait_recv()
        fsend[t, 2, 80:144] = (
            fsend[t, 2, 80:144].astype(F32) + frelay[t, 80:144].astype(F32)
        ).astype(BF16)
        hop(t, 5).start()
    grad_normed = dot(grad_proj, wqkv[...], (1, 0))
    x_hat = xhat[...]
    first = jnp.mean(grad_normed, axis=-1, keepdims=True)
    second = jnp.mean(grad_normed * x_hat, axis=-1, keepdims=True)
    wide[...] = (grad_normed - first - x_hat * second) * inv_std
    pack(wide, gbs)
    push_all(gbs, gbr, gb_ss, gb_rs)

    def cross(t, k):
        to = (ring[1 - t] + k) % 4
        return remote(
            hsend.at[t, to], hrecv.at[t, ring[1 - t]], h_ss.at[t, to], h_rs.at[t, ring[1 - t]],
            dp, member(1 - t, to),
        )

    for t in range(2):
        for n in range(2, 6):
            hop(t, n).wait_recv()
        own[t, 0:144] += fback[t, 0].astype(F32) + fback[t, 1].astype(F32)
        for p in range(4):
            hsend[t, p] = own[t, 36 * p : 36 * p + 48].astype(BF16)
        for k in (2, 1, 3):
            cross(t, k).start()
        hrecv[t, ring[1 - t]] = hsend[t, ring[1 - t]]

    sent_all(xs, xr, x_ss, x_rs)
    sent_all(gs, gr, g_ss, g_rs)
    sent_all(ats, atr, at_ss, at_rs)
    swap_cot.wait_send()
    swap_a.wait_send()
    swap_g.wait_send()
    swap_t.wait_send()
    z_take(wsend, wrecv, w_ss, w_rs)
    total = wrecv[0].astype(F32)
    for n in range(1, 8):
        total = total + wrecv[n].astype(F32)
    wsum[0:144, :] = total
    wsum[144:160, :] = jnp.zeros((16, 288), F32)
    for n in range(16):
        begin = (n // 2) * 18
        vsend[n] = wsum[begin : begin + 32, 144 * (n % 2) : 144 * (n % 2) + 144].astype(BF16)

    def v_target(n):
        return z_hi * 2 + n % 2, z_lo * PLANE + 8 * core + n // 2

    @pl.loop(0, 16)
    def _(n):
        to_dp, to_seq = v_target(n)
        own = (to_dp == dp) & (to_seq == seq)

        @pl.when(own)
        def _():
            vrecv[xy] = vsend[n]

        @pl.when(jnp.logical_not(own))
        def _():
            remote(vsend.at[n], vrecv.at[xy], v_ss.at[n], v_rs.at[xy], to_dp, to_seq).start()

    for t in range(2):
        for k in range(1, 4):
            come = (ring[1 - t] + k) % 4
            remote(
                hsend.at[t, come], hrecv.at[t, come], h_ss.at[t, come], h_rs.at[t, come],
                dp, member(1 - t, come),
            ).wait_recv()
        total = hrecv[t, 0].astype(F32)
        for p in range(1, 4):
            total = total + hrecv[t, p].astype(F32)
        for j in range(4):
            zsend[2 * j + t] = total[:, 216 * j : 216 * j + 216].astype(BF16)
    z_push(zsend, zrecv, z_ss, z_rs)

    take_all(gbs, gbr, gb_ss, gb_rs)
    unpack(gbr, wide)
    ordered = dot(move, wide[...].astype(BF16), (0, 0))
    gtok[...] = (cot[...].astype(F32) + ordered).astype(BF16)

    @pl.loop(0, 16)
    def _(n):
        from_dp, from_seq = z_hi * 2 + xy // 8, z_lo * PLANE + n

        @pl.when(jnp.logical_not((from_dp == dp) & (from_seq == seq)))
        def _():
            remote(vsend.at[n], vrecv.at[n], v_ss.at[n], v_rs.at[n], from_dp, from_seq).wait_recv()

    total = vrecv[0].astype(F32)
    for n in range(1, 16):
        total = total + vrecv[n].astype(F32)
    gwo[...] = total[:18, :] * FACTOR

    z_take(zsend, zrecv, z_ss, z_rs)
    total = zrecv[0].astype(F32)
    for n in range(1, 8):
        total = total + zrecv[n].astype(F32)
    gwq[...] = total[:36, :] * FACTOR

    sent_all(gbs, gbr, gb_ss, gb_rs)
    for t in range(2):
        for n in range(6):
            hop(t, n).wait_send()
        for k in range(1, 4):
            cross(t, k).wait_send()

    z_sent(wsend, wrecv, w_ss, w_rs)
    z_sent(zsend, zrecv, z_ss, z_rs)

    @pl.loop(0, 16)
    def _(n):
        to_dp, to_seq = v_target(n)

        @pl.when(jnp.logical_not((to_dp == dp) & (to_seq == seq)))
        def _():
            remote(vsend.at[n], vrecv.at[n], v_ss.at[n], v_rs.at[n], to_dp, to_seq).wait_send()


def hand_over(*refs):
    for n in range(4):
        refs[4 + n][...] = refs[n][...]


def shards(tokens, cotangent, w_qkv, w_out):
    shape = tokens.shape
    vmem = pl.BlockSpec(memory_space=pltpu.VMEM)
    hbm = pl.BlockSpec(memory_space=pl.ANY)
    dma = pltpu.SemaphoreType.DMA
    scratch = [
        ((3 * HD, D), BF16), ((HD, D), BF16),
        ((ROWS, D), F32), ((ROWS, HD), F32), ((ROWS, D), F32), ((ROWS, D), BF16),
        ((SEQ, 4, D), BF16), ((SEQ, 4, D), BF16), ((SEQ, 4, HD), BF16), ((SEQ, 4, HD), BF16),
        ((SEQ, 4, HD), BF16), ((SEQ, 4, HD), BF16), ((SEQ, 4, D), BF16), ((SEQ, 4, D), BF16),
        ((4, ROWS, 288), BF16), ((2, ROWS, 288), BF16),
        ((D, ROWS), F32), ((D, ROWS), F32), ((D, ROWS), BF16), ((D, ROWS), BF16),
        ((2, ROWS, 864), BF16), ((ROWS, 864), BF16), ((HD, ROWS), BF16), ((HD, ROWS), BF16),
        ((HEADS * ROWS, HD), BF16), ((HEADS * ROWS, HD), BF16),
        ((HEADS * ROWS, HD), BF16), ((HEADS * ROWS, HD), BF16),
        ((HEADS * ROWS, ROWS), F32), ((HEADS * ROWS, ROWS), BF16),
        ((2, 3, 144, 864), BF16), ((2, 144, 864), BF16), ((2, 2, 144, 864), BF16), ((2, 160, 864), F32),
        ((2, 4, 48, 864), BF16), ((2, 4, 48, 864), BF16),
        ((8, 48, 216), BF16), ((8, 48, 216), BF16),
        ((8, 144, 288), BF16), ((8, 144, 288), BF16), ((160, 288), F32),
        ((16, 32, 144), BF16), ((16, 32, 144), BF16),
    ]
    sems = [(2,)] + [(SEQ,)] * 8 + [(4,)] * 2 + [(2, 6)] * 2 + [(2, 4)] * 2 + [(8,)] * 4 + [(16,)] * 2
    out_shape = (
        jax.ShapeDtypeStruct((ROWS, D), BF16),
        jax.ShapeDtypeStruct((ROWS, D), BF16),
        jax.ShapeDtypeStruct((36, 216), F32),
        jax.ShapeDtypeStruct((18, 144), F32),
    )
    outs = pl.pallas_call(
        kernel,
        out_shape=out_shape,
        in_specs=[vmem, vmem, hbm, hbm],
        out_specs=(vmem,) * 4,
        scratch_shapes=[pltpu.VMEM(s, t) for s, t in scratch] + [dma(n) for n in sems],
        compiler_params=pltpu.CompilerParams(
            collective_id=0, has_side_effects=True, vmem_limit_bytes=56 * 1024 * 1024
        ),
    )(tokens.reshape(ROWS, D), cotangent.reshape(ROWS, D), w_qkv.T, w_out)
    result, gtok, gwq, gwo = pl.pallas_call(
        hand_over,
        out_shape=out_shape,
        in_specs=[vmem] * 4,
        out_specs=(vmem,) * 4,
    )(*outs)
    return (result.reshape(shape), gtok.reshape(shape), gwq, gwo)


def solution(mesh):
    in_specs = (P("dp", "seq", None, None), P("dp", "seq", None, None), P(), P())
    out_specs = (
        P("dp", "seq", None, None),
        P("dp", "seq", None, None),
        P("seq", "dp"),
        P("seq", "dp"),
    )
    return jax.shard_map(shards, mesh=mesh, in_specs=in_specs, out_specs=out_specs, check_vma=False)
```

```python
import functools

import jax
import jax.numpy as jnp
from jax import lax
from jax.experimental import pallas as pl
from jax.experimental.pallas import tpu as pltpu
from jax.sharding import PartitionSpec as P

MESH = pl.DeviceIdType.MESH
F32, BF16 = jnp.float32, jnp.bfloat16

D = 1152
HEADS = 8
HS = 72
HD = 576
ROWS = 128
SEQ = 32
PLANE = 16
EPS = 1e-6
SCALE = HS ** (-0.5)
FACTOR = 32768 ** (-0.5)


def dot(a, b, contract):
    return lax.dot_general(a, b, ((contract[:1], contract[1:]), ((), ())), preferred_element_type=F32)


def kernel(
    tok_hbm, cot_hbm, wqkv_hbm, wout_hbm,
    result_hbm, gtok_hbm, gwq, gwo,
    tok, cot, wqkv, wout, result, gtok,
    wide, slim, xhat, cotp,
    xs, xr, gs, gr, ats, atr, gbs, gbr,
    cots, cotr, ntr, arr, amine, apart, gph, gpart, ttr, tarr, tmine, tpart,
    qb, kb, vb, gab, probs, plow,
    fsend0, frelay0, fback0, own0, fsend1, frelay1, fback1, own1, hsend, hrecv, zsend, zrecv,
    wsem, a_ss, a_rs, c_ss, c_rs, f_ss, f_rs, h_ss, h_rs, z_ss, z_rs,
):
    dp, seq = lax.axis_index("dp"), lax.axis_index("seq")
    core, z_hi = dp % 2, dp // 2
    xy, z_lo = seq % PLANE, seq // PLANE
    mate = z_hi * 2 + 1 - core
    zed = z_hi * 2 + z_lo
    x, y = xy % 4, xy // 4
    step = 1 + 2 * core

    def remote(src, dst, send_sem, recv_sem, to_dp, to_seq):
        return pltpu.make_async_remote_copy(
            src_ref=src, dst_ref=dst, send_sem=send_sem, recv_sem=recv_sem,
            device_id=(to_dp, to_seq), device_id_type=MESH,
        )

    barrier = pltpu.get_barrier_semaphore()

    def greet(to_dp, to_seq):
        pl.semaphore_signal(barrier, inc=1, device_id=(to_dp, to_seq), device_id_type=MESH)

    @pl.loop(1, SEQ)
    def _(k):
        greet(dp, (seq + k) % SEQ)

    @pl.loop(1, 8)
    def _(k):
        greet((dp + k) % 8, xy)
        greet((dp + k) % 8, PLANE + xy)

    load_wqkv = pltpu.make_async_copy(wqkv_hbm, wqkv, wsem.at[0])
    load_wout = pltpu.make_async_copy(wout_hbm, wout, wsem.at[1])
    load_tok = pltpu.make_async_copy(tok_hbm, tok, wsem.at[2])
    load_cot = pltpu.make_async_copy(cot_hbm, cot, wsem.at[3])
    load_tok.start()
    load_cot.start()
    load_wout.start()
    load_wqkv.start()

    new = lax.broadcasted_iota(jnp.int32, (ROWS, ROWS), 0)
    old = lax.broadcasted_iota(jnp.int32, (ROWS, ROWS), 1)
    place = ((new >> 1) & 1) * 64 + (new >> 2) * 2 + (new & 1)
    move = jnp.where(place == old, 1.0, 0.0).astype(BF16)

    def pack(rows, block):
        for p in range(SEQ):
            block[p] = rows[4 * p : 4 * p + 4, :].astype(BF16)

    def unpack(block, rows):
        for p in range(SEQ):
            rows[4 * p : 4 * p + 4, :] = block[p].astype(F32)

    def push_all(src, dst, e):
        @pl.loop(1, SEQ)
        def _(k):
            to = (seq + k) % SEQ
            remote(src.at[to], dst.at[seq], a_ss.at[e], a_rs.at[e], dp, to).start()

        pltpu.make_async_copy(src.at[seq], dst.at[seq], a_rs.at[e]).start()

    def take_all(src, dst, e):
        pltpu.make_async_copy(src, dst, a_rs.at[e]).wait()

    def sent_all(src, dst, e):
        many = pl.ds(0, SEQ - 1)
        remote(src.at[many], dst.at[many], a_ss.at[e], a_rs.at[e], dp, (seq + 1) % SEQ).wait_send()

    load_tok.wait()
    wide[...] = dot(move, tok[...], (1, 0))
    pack(wide, xs)
    pl.semaphore_wait(barrier, SEQ - 1 + 14)
    push_all(xs, xr, 0)

    load_cot.wait()
    cotp[...] = dot(move, cot[...], (1, 0)).astype(BF16)
    load_wout.wait()
    slim[...] = dot(cotp[...], wout[...], (1, 1))
    pack(slim, gs)
    push_all(gs, gr, 1)
    for c in range(2):
        half = cotp[:, HD * c : HD * c + HD].astype(F32)
        gap0, gap1 = jnp.zeros((ROWS, 72), F32), jnp.zeros((ROWS, 144), F32)
        whole, left, right = [], [], []
        for j in range(4):
            b = 144 * j
            whole += [half[:, b : b + 144], gap0]
            left += [gap1, half[:, b : b + 72]]
            right += [gap1, half[:, b + 72 : b + 144]]
        for n, parts in enumerate((whole, left, right)):
            cots[c, n * ROWS : (n + 1) * ROWS, :] = jnp.concatenate(parts, axis=1).astype(BF16)
    swap_cot = remote(cots.at[1 - core], cotr, c_ss.at[0], c_rs.at[0], mate, seq)
    swap_cot.start()

    take_all(xs, xr, 0)
    unpack(xr, wide)
    moved = wide[...]
    centered = moved - jnp.mean(moved, axis=-1, keepdims=True)
    inv_std = lax.rsqrt(jnp.mean(centered * centered, axis=-1, keepdims=True) + EPS)
    x_hat = centered * inv_std
    xhat[...] = x_hat
    load_wqkv.wait()
    normed = x_hat.astype(BF16)
    query = dot(normed, wqkv[0:HD, :], (1, 1)).astype(BF16)
    key = dot(normed, wqkv[HD : 2 * HD, :], (1, 1)).astype(BF16)
    value = dot(normed, wqkv[2 * HD : 3 * HD, :], (1, 1)).astype(BF16)
    lane = lax.broadcasted_iota(jnp.int32, (ROWS, HD), 1)

    def stack(block, out):
        wide_block = block.astype(F32)
        for h in range(HEADS):
            inside = (lane >= h * HS) & (lane < (h + 1) * HS)
            out[h * ROWS : (h + 1) * ROWS, :] = jnp.where(inside, wide_block, 0.0).astype(BF16)

    def side(block):
        return jnp.concatenate([block[h * ROWS : (h + 1) * ROWS, :] for h in range(HEADS)], axis=1)

    stack(query, qb)
    stack(value, vb)
    scores = dot(qb[...], key, (1, 1)) * SCALE
    here = lax.broadcasted_iota(jnp.int32, (HEADS * ROWS, ROWS), 0)
    there = lax.broadcasted_iota(jnp.int32, (HEADS * ROWS, ROWS), 1)
    scores = jnp.where(((here ^ there) & 1) == 0, scores, -jnp.inf)
    expo = jnp.exp(scores - jnp.max(scores, axis=-1, keepdims=True))
    prob = expo / jnp.sum(expo, axis=-1, keepdims=True)
    probs[...] = prob
    plow[...] = prob.astype(BF16)
    slim[...] = dot(side(plow), vb[...], (1, 0))
    pack(slim, ats)
    push_all(ats, atr, 2)

    ntr[...] = xhat[...].T
    for p in range(PLANE):
        begin = 144 * (p % 4) + 36 * (p // 4)
        arr[begin : begin + 36, :] = ntr[36 * p : 36 * p + 36, :]
    arr[576:, :] = ntr[576:, :]
    amine[...] = arr[...].astype(BF16)
    swap_a = remote(amine, apart, c_ss.at[1], c_rs.at[1], mate, seq)
    swap_a.start()

    stack(key, kb)
    take_all(gs, gr, 1)
    unpack(gr, slim)
    stack(slim[...], gab)
    grad_probs = dot(gab[...], value, (1, 1))
    prob = probs[...]
    delta = jnp.sum(prob * grad_probs, axis=-1, keepdims=True)
    grad_scores = (prob * (grad_probs - delta) * SCALE).astype(BF16)
    grad_query = dot(side(grad_scores), kb[...], (1, 0))
    grad_key = dot(grad_scores, qb[...], (0, 0))
    grad_value = dot(plow[...], gab[...], (0, 0))
    grad_proj = jnp.concatenate([grad_query, grad_key, grad_value], axis=1)
    gph[0] = grad_proj[:, :864].astype(BF16)
    gph[1] = grad_proj[:, 864:].astype(BF16)
    swap_g = remote(gph.at[1 - core], gpart, c_ss.at[2], c_rs.at[2], mate, seq)
    swap_g.start()
    grad_proj = grad_proj.astype(BF16)

    grad_normed = dot(grad_proj, wqkv[...], (1, 0))
    x_hat = xhat[...]
    first = jnp.mean(grad_normed, axis=-1, keepdims=True)
    second = jnp.mean(grad_normed * x_hat, axis=-1, keepdims=True)
    wide[...] = (grad_normed - first - x_hat * second) * inv_std
    pack(wide, gbs)
    swap_a.wait_recv()
    swap_g.wait_recv()

    size, part, piece = (144, 48), (80, 32), (36, 12)
    fsend, frelay, fback, own = (fsend0, fsend1), (frelay0, frelay1), (fback0, fback1), (own0, own1)
    ring = (x, y)

    def member(t, r):
        r = r % 4
        return z_lo * PLANE + (4 * y + r if t == 0 else 4 * r + x)

    def block(kind, t, to):
        mine, theirs = ((amine, apart), (tmine, tpart))[kind]
        n = size[kind]
        rows = pl.ds(pl.multiple_of((t * 4 + to) * n, 16), n)
        if kind == 0:
            right = jnp.concatenate([gph[core], gpart[...]], axis=0)
        else:
            right = jnp.concatenate([cots[core], cotr[...]], axis=0)
        return dot(jnp.concatenate([mine[rows, :], theirs[rows, :]], axis=1), right, (1, 0))

    def hop(kind, t, n):
        send, relay, back = fsend[kind], frelay[kind], fback[kind]
        half = (slice(0, part[kind]), slice(part[kind], size[kind]))[n % 2]
        dst = relay.at[t, half] if n < 2 else back.at[t, n // 2 - 1, half]
        ahead = n in (0, 2, 3)
        to = ring[t] + (step if ahead else 4 - step)
        return remote(
            send.at[t, n // 2, half], dst, f_ss.at[kind, t, n], f_rs.at[kind, t, n], dp, member(t, to)
        )

    def opposite(kind):
        for t in range(2):
            fsend[kind][t, 0] = block(kind, t, (ring[t] + 2) % 4).astype(BF16)
            hop(kind, t, 0).start()
            hop(kind, t, 1).start()

    def near(kind):
        for t in range(2):
            fsend[kind][t, 1] = block(kind, t, (ring[t] + step) % 4).astype(BF16)
            hop(kind, t, 3).start()
            fsend[kind][t, 2] = block(kind, t, (ring[t] + 4 - step) % 4).astype(BF16)
            hop(kind, t, 4).start()

    def stay(kind):
        for t in range(2):
            own[kind][t] = block(kind, t, ring[t])

    def relays(kind):
        send, relay, cut = fsend[kind], frelay[kind], part[kind]
        for t in range(2):
            for n, half in ((0, slice(0, cut)), (1, slice(cut, size[kind]))):
                hop(kind, t, n).wait_recv()
                send[t, 1 + n, half] = (
                    send[t, 1 + n, half].astype(F32) + relay[t, half].astype(F32)
                ).astype(BF16)
                hop(kind, t, 2 + 3 * n).start()

    def arrived(kind):
        for t in range(2):
            for n in range(2, 6):
                hop(kind, t, n).wait_recv()
            own[kind][t] += fback[kind][t, 0].astype(F32) + fback[kind][t, 1].astype(F32)

    def cross():
        for t in range(2):
            here = ring[1 - t]
            for p in range(4):
                hsend[t, p] = jnp.concatenate(
                    [own0[t, 36 * p : 36 * p + 36], own1[t, 12 * p : 12 * p + 12]], axis=0
                ).astype(BF16)
            for k in (2, 1, 3):
                to = (here + k) % 4
                remote(
                    hsend.at[t, to], hrecv.at[t, here], h_ss.at[t], h_rs.at[t], dp, member(1 - t, to)
                ).start()
            pltpu.make_async_copy(hsend.at[t, here], hrecv.at[t, here], h_rs.at[t]).start()

    def z_target(n):
        return 4 * core + n // 2, (n % 2) * PLANE + xy

    def crossed():
        for t in range(2):
            pltpu.make_async_copy(hsend.at[t], hrecv.at[t], h_rs.at[t]).wait()
            total = hrecv[t, 0].astype(F32)
            for p in range(1, 4):
                total = total + hrecv[t, p].astype(F32)
            for j in range(4):
                zsend[2 * j + t] = total[:, 216 * j : 216 * j + 216].astype(BF16)

        @pl.loop(0, 8)
        def _(n):
            to_dp, to_seq = z_target(n)
            is_me = (to_dp == dp) & (to_seq == seq)

            @pl.when(is_me)
            def _():
                pltpu.make_async_copy(zsend.at[n], zrecv.at[zed], z_rs.at[0]).start()

            @pl.when(jnp.logical_not(is_me))
            def _():
                remote(zsend.at[n], zrecv.at[zed], z_ss.at[0], z_rs.at[0], to_dp, to_seq).start()

    def gathered():
        pltpu.make_async_copy(zsend, zrecv, z_rs.at[0]).wait()
        total = zrecv[0].astype(F32)
        for n in range(1, 8):
            total = total + zrecv[n].astype(F32)
        return total * FACTOR

    def z_sent(count):
        many = pl.ds(0, count)
        remote(
            zsend.at[many], zrecv.at[many], z_ss.at[0], z_rs.at[0], mate, seq
        ).wait_send()

    def all_sent():
        for t in range(2):
            for kind in range(2):
                for n in range(6):
                    hop(kind, t, n).wait_send()
            many = pl.ds(0, 3)
            remote(
                hsend.at[t, many], hrecv.at[t, many], h_ss.at[t], h_rs.at[t], dp, member(1 - t, ring[1 - t] + 1)
            ).wait_send()
        pl.when(z_hi // 2 == core)(lambda: z_sent(7))
        pl.when(z_hi // 2 != core)(lambda: z_sent(8))

    opposite(0)
    near(0)
    take_all(ats, atr, 2)
    unpack(atr, slim)
    ttr[...] = slim[...].T
    tarr[...] = jnp.zeros((384, 3 * ROWS), F32)
    for p in range(2 * PLANE):
        if p < PLANE:
            begin = 48 * (p % 4) + 12 * (p // 4)
        else:
            begin = 12 * p
        tarr[begin : begin + 12, 0:ROWS] = ttr[18 * p : 18 * p + 12, :]
        rest = ttr[18 * p + 12 : 18 * p + 18, :]
        tarr[begin : begin + 6, ROWS : 2 * ROWS] = rest
        tarr[begin + 6 : begin + 12, 2 * ROWS :] = rest
    tmine[...] = tarr[...].astype(BF16)
    swap_t = remote(tmine, tpart, c_ss.at[3], c_rs.at[3], mate, seq)
    swap_t.start()
    stay(0)
    swap_cot.wait_recv()
    swap_t.wait_recv()
    opposite(1)
    relays(0)
    near(1)
    ordered = dot(move, slim[...].astype(BF16), (0, 0)).astype(BF16)
    branch = dot(ordered, wout[...], (1, 0))
    result[...] = (tok[...].astype(F32) + branch).astype(BF16)
    store_result = pltpu.make_async_copy(result, result_hbm, wsem.at[4])
    store_result.start()
    relays(1)
    stay(1)
    sent_all(xs, xr, 0)
    sent_all(gs, gr, 1)
    sent_all(ats, atr, 2)
    swap_cot.wait_send()
    swap_a.wait_send()
    swap_g.wait_send()
    swap_t.wait_send()
    arrived(0)
    arrived(1)
    cross()
    push_all(gbs, gbr, 3)
    crossed()
    take_all(gbs, gbr, 3)
    unpack(gbr, wide)
    ordered = dot(move, wide[...].astype(BF16), (0, 0))
    gtok[...] = (cot[...].astype(F32) + ordered).astype(BF16)
    store_gtok = pltpu.make_async_copy(gtok, gtok_hbm, wsem.at[5])
    store_gtok.start()
    sent_all(gbs, gbr, 3)
    owned = gathered()
    gwq[...] = owned[:36, :]
    gwo[0:12, :] = owned[36:48, 0:144]
    gwo[12:18, :] = jnp.concatenate([owned[36:42, 144:216], owned[42:48, 144:216]], axis=1)
    all_sent()
    store_result.wait()
    store_gtok.wait()


def hand_over(*refs):
    for n in range(4):
        refs[4 + n][...] = refs[n][...]


def shards(tokens, cotangent, w_qkv, w_out):
    shape = tokens.shape
    vmem = pl.BlockSpec(memory_space=pltpu.VMEM)
    hbm = pl.BlockSpec(memory_space=pl.ANY)
    dma = pltpu.SemaphoreType.DMA
    scratch = [
        ((ROWS, D), BF16), ((ROWS, D), BF16), ((3 * HD, D), BF16), ((HD, D), BF16),
        ((ROWS, D), BF16), ((ROWS, D), BF16),
        ((ROWS, D), F32), ((ROWS, HD), F32), ((ROWS, D), F32), ((ROWS, D), BF16),
        ((SEQ, 4, D), BF16), ((SEQ, 4, D), BF16), ((SEQ, 4, HD), BF16), ((SEQ, 4, HD), BF16),
        ((SEQ, 4, HD), BF16), ((SEQ, 4, HD), BF16), ((SEQ, 4, D), BF16), ((SEQ, 4, D), BF16),
        ((2, 3 * ROWS, 864), BF16), ((3 * ROWS, 864), BF16),
        ((D, ROWS), F32), ((D, ROWS), F32), ((D, ROWS), BF16), ((D, ROWS), BF16),
        ((2, ROWS, 864), BF16), ((ROWS, 864), BF16), ((HD, ROWS), F32), ((384, 3 * ROWS), F32), ((384, 3 * ROWS), BF16), ((384, 3 * ROWS), BF16),
        ((HEADS * ROWS, HD), BF16), ((HEADS * ROWS, HD), BF16),
        ((HEADS * ROWS, HD), BF16), ((HEADS * ROWS, HD), BF16),
        ((HEADS * ROWS, ROWS), F32), ((HEADS * ROWS, ROWS), BF16),
        ((2, 3, 144, 864), BF16), ((2, 144, 864), BF16), ((2, 2, 144, 864), BF16), ((2, 144, 864), F32),
        ((2, 3, 48, 864), BF16), ((2, 48, 864), BF16), ((2, 2, 48, 864), BF16), ((2, 48, 864), F32),
        ((2, 4, 48, 864), BF16), ((2, 4, 48, 864), BF16), ((8, 48, 216), BF16), ((8, 48, 216), BF16),
    ]
    sems = [(6,), (4,), (4,), (4,), (4,), (2, 2, 6), (2, 2, 6), (2,), (2,), (1,), (1,)]
    out_shape = (
        jax.ShapeDtypeStruct((ROWS, D), BF16),
        jax.ShapeDtypeStruct((ROWS, D), BF16),
        jax.ShapeDtypeStruct((36, 216), F32),
        jax.ShapeDtypeStruct((18, 144), F32),
    )
    outs = pl.pallas_call(
        kernel,
        out_shape=out_shape,
        in_specs=[hbm] * 4,
        out_specs=(hbm, hbm, vmem, vmem),
        scratch_shapes=[pltpu.VMEM(s, t) for s, t in scratch] + [dma(n) for n in sems],
        compiler_params=pltpu.CompilerParams(
            collective_id=0, has_side_effects=True, vmem_limit_bytes=56 * 1024 * 1024
        ),
    )(tokens.reshape(ROWS, D), cotangent.reshape(ROWS, D), w_qkv.T, w_out)
    result, gtok, gwq, gwo = pl.pallas_call(
        hand_over,
        out_shape=out_shape,
        in_specs=[vmem] * 4,
        out_specs=(vmem,) * 4,
    )(*outs)
    return (result.reshape(shape), gtok.reshape(shape), gwq, gwo)


def solution(mesh):
    in_specs = (P("dp", "seq", None, None), P("dp", "seq", None, None), P(), P())
    out_specs = (
        P("dp", "seq", None, None),
        P("dp", "seq", None, None),
        P("seq", "dp"),
        P("seq", "dp"),
    )
    return jax.shard_map(shards, mesh=mesh, in_specs=in_specs, out_specs=out_specs, check_vma=False)
```

```python
import functools

import jax
import jax.numpy as jnp
from jax import lax
from jax.experimental import pallas as pl
from jax.experimental.pallas import tpu as pltpu
from jax.sharding import PartitionSpec as P

MESH = pl.DeviceIdType.MESH
F32, BF16 = jnp.float32, jnp.bfloat16

D = 1152
HEADS = 8
HS = 72
HD = 576
ROWS = 128
SEQ = 32
PLANE = 16
EPS = 1e-6
SCALE = HS ** (-0.5)
FACTOR = 32768 ** (-0.5)


def dot(a, b, contract):
    return lax.dot_general(a, b, ((contract[:1], contract[1:]), ((), ())), preferred_element_type=F32)


def kernel(
    tok_hbm, cot_hbm, wqkv_hbm, wout_hbm,
    result_hbm, gtok_hbm, gwq, gwo,
    tok, cot, wqkv, wout, result, gtok,
    wide, slim, xhat, cotp,
    xs, xr, gs, gr, ats, atr, gbs, gbr,
    cots, cotr, ntr, arr, amine, apart, gph, gpart, ttr, tarr, tmine, tpart,
    qb, kb, vb, gab, probs, plow,
    fsend0, frelay0, fback0, own0, fsend1, frelay1, fback1, own1, hsend, hrecv, zsend, zrecv,
    wsem, a_ss, a_rs, c_ss, c_rs, f_ss, f_rs, h_ss, h_rs, z_ss, z_rs,
):
    dp, seq = lax.axis_index("dp"), lax.axis_index("seq")
    core, z_hi = dp % 2, dp // 2
    xy, z_lo = seq % PLANE, seq // PLANE
    mate = z_hi * 2 + 1 - core
    zed = z_hi * 2 + z_lo
    x, y = xy % 4, xy // 4
    step = 1 + 2 * core

    def remote(src, dst, send_sem, recv_sem, to_dp, to_seq):
        return pltpu.make_async_remote_copy(
            src_ref=src, dst_ref=dst, send_sem=send_sem, recv_sem=recv_sem,
            device_id=(to_dp, to_seq), device_id_type=MESH,
        )

    barrier = pltpu.get_barrier_semaphore()

    def greet(to_dp, to_seq):
        pl.semaphore_signal(barrier, inc=1, device_id=(to_dp, to_seq), device_id_type=MESH)

    @pl.loop(1, SEQ)
    def _(k):
        greet(dp, (seq + k) % SEQ)

    @pl.loop(1, 8)
    def _(k):
        greet((dp + k) % 8, xy)
        greet((dp + k) % 8, PLANE + xy)

    load_wqkv = pltpu.make_async_copy(wqkv_hbm, wqkv, wsem.at[0])
    load_wout = pltpu.make_async_copy(wout_hbm, wout, wsem.at[1])
    load_tok = pltpu.make_async_copy(tok_hbm, tok, wsem.at[2])
    load_cot = pltpu.make_async_copy(cot_hbm, cot, wsem.at[3])
    load_tok.start()
    load_cot.start()
    load_wout.start()
    load_wqkv.start()

    new = lax.broadcasted_iota(jnp.int32, (ROWS, ROWS), 0)
    old = lax.broadcasted_iota(jnp.int32, (ROWS, ROWS), 1)
    place = ((new >> 1) & 1) * 64 + (new >> 2) * 2 + (new & 1)
    move = jnp.where(place == old, 1.0, 0.0).astype(BF16)

    def pack(rows, block):
        for p in range(SEQ):
            block[p] = rows[4 * p : 4 * p + 4, :].astype(BF16)

    def unpack(block, rows):
        for p in range(SEQ):
            rows[4 * p : 4 * p + 4, :] = block[p].astype(F32)

    def push_all(src, dst, e):
        @pl.loop(1, SEQ)
        def _(k):
            to = (seq + k) % SEQ
            remote(src.at[to], dst.at[seq], a_ss.at[e], a_rs.at[e], dp, to).start()

        pltpu.make_async_copy(src.at[seq], dst.at[seq], a_rs.at[e]).start()

    def take_all(src, dst, e):
        pltpu.make_async_copy(src, dst, a_rs.at[e]).wait()

    def sent_all(src, dst, e):
        many = pl.ds(0, SEQ - 1)
        remote(src.at[many], dst.at[many], a_ss.at[e], a_rs.at[e], dp, (seq + 1) % SEQ).wait_send()

    load_tok.wait()
    wide[...] = dot(move, tok[...], (1, 0))
    pack(wide, xs)
    pl.semaphore_wait(barrier, SEQ - 1 + 14)
    push_all(xs, xr, 0)

    load_cot.wait()
    cotp[...] = dot(move, cot[...], (1, 0)).astype(BF16)
    load_wout.wait()
    slim[...] = dot(cotp[...], wout[...], (1, 1))
    pack(slim, gs)
    push_all(gs, gr, 1)
    for c in range(2):
        half = cotp[:, HD * c : HD * c + HD].astype(F32)
        gap0, gap1 = jnp.zeros((ROWS, 72), F32), jnp.zeros((ROWS, 144), F32)
        whole, left, right = [], [], []
        for j in range(4):
            b = 144 * j
            whole += [half[:, b : b + 144], gap0]
            left += [gap1, half[:, b : b + 72]]
            right += [gap1, half[:, b + 72 : b + 144]]
        for n, parts in enumerate((whole, left, right)):
            cots[c, n * ROWS : (n + 1) * ROWS, :] = jnp.concatenate(parts, axis=1).astype(BF16)
    swap_cot = remote(cots.at[1 - core], cotr, c_ss.at[0], c_rs.at[0], mate, seq)
    swap_cot.start()

    take_all(xs, xr, 0)
    unpack(xr, wide)
    moved = wide[...]
    centered = moved - jnp.mean(moved, axis=-1, keepdims=True)
    inv_std = lax.rsqrt(jnp.mean(centered * centered, axis=-1, keepdims=True) + EPS)
    x_hat = centered * inv_std
    xhat[...] = x_hat
    load_wqkv.wait()
    normed = x_hat.astype(BF16)
    query = dot(normed, wqkv[0:HD, :], (1, 1)).astype(BF16)
    key = dot(normed, wqkv[HD : 2 * HD, :], (1, 1)).astype(BF16)
    value = dot(normed, wqkv[2 * HD : 3 * HD, :], (1, 1)).astype(BF16)
    lane = lax.broadcasted_iota(jnp.int32, (ROWS, HD), 1)

    def stack(block, out):
        wide_block = block.astype(F32)
        for h in range(HEADS):
            inside = (lane >= h * HS) & (lane < (h + 1) * HS)
            out[h * ROWS : (h + 1) * ROWS, :] = jnp.where(inside, wide_block, 0.0).astype(BF16)

    def side(block):
        return jnp.concatenate([block[h * ROWS : (h + 1) * ROWS, :] for h in range(HEADS)], axis=1)

    stack(query, qb)
    stack(value, vb)
    scores = dot(qb[...], key, (1, 1)) * SCALE
    here = lax.broadcasted_iota(jnp.int32, (HEADS * ROWS, ROWS), 0)
    there = lax.broadcasted_iota(jnp.int32, (HEADS * ROWS, ROWS), 1)
    scores = jnp.where(((here ^ there) & 1) == 0, scores, -jnp.inf)
    expo = jnp.exp(scores - jnp.max(scores, axis=-1, keepdims=True))
    prob = expo / jnp.sum(expo, axis=-1, keepdims=True)
    probs[...] = prob
    plow[...] = prob.astype(BF16)
    slim[...] = dot(side(plow), vb[...], (1, 0))
    pack(slim, ats)
    push_all(ats, atr, 2)

    ntr[...] = xhat[...].T
    for p in range(PLANE):
        begin = 144 * (p % 4) + 36 * (p // 4)
        arr[begin : begin + 36, :] = ntr[36 * p : 36 * p + 36, :]
    arr[576:, :] = ntr[576:, :]
    amine[...] = arr[...].astype(BF16)
    swap_a = remote(amine, apart, c_ss.at[1], c_rs.at[1], mate, seq)
    swap_a.start()

    stack(key, kb)
    take_all(gs, gr, 1)
    unpack(gr, slim)
    stack(slim[...], gab)
    grad_probs = dot(gab[...], value, (1, 1))
    prob = probs[...]
    delta = jnp.sum(prob * grad_probs, axis=-1, keepdims=True)
    grad_scores = (prob * (grad_probs - delta) * SCALE).astype(BF16)
    grad_query = dot(side(grad_scores), kb[...], (1, 0))
    grad_key = dot(grad_scores, qb[...], (0, 0))
    grad_value = dot(plow[...], gab[...], (0, 0))
    grad_proj = jnp.concatenate([grad_query, grad_key, grad_value], axis=1)
    gph[0] = grad_proj[:, :864].astype(BF16)
    gph[1] = grad_proj[:, 864:].astype(BF16)
    swap_g = remote(gph.at[1 - core], gpart, c_ss.at[2], c_rs.at[2], mate, seq)
    swap_g.start()
    grad_proj = grad_proj.astype(BF16)

    grad_normed = dot(grad_proj, wqkv[...], (1, 0))
    x_hat = xhat[...]
    first = jnp.mean(grad_normed, axis=-1, keepdims=True)
    second = jnp.mean(grad_normed * x_hat, axis=-1, keepdims=True)
    wide[...] = (grad_normed - first - x_hat * second) * inv_std
    pack(wide, gbs)

    def push_rows(to):
        remote(gbs.at[to], gbr.at[seq], a_ss.at[3], a_rs.at[3], dp, to).start()

    @pl.loop(0, PLANE)
    def _(k):
        push_rows((1 - z_lo) * PLANE + (xy + k) % PLANE)

    swap_a.wait_recv()
    swap_g.wait_recv()

    size, part, piece = (144, 48), (80, 32), (36, 12)
    fsend, frelay, fback, own = (fsend0, fsend1), (frelay0, frelay1), (fback0, fback1), (own0, own1)
    ring = (x, y)

    def member(t, r):
        r = r % 4
        return z_lo * PLANE + (4 * y + r if t == 0 else 4 * r + x)

    def block(kind, t, to):
        mine, theirs = ((amine, apart), (tmine, tpart))[kind]
        n = size[kind]
        rows = pl.ds(pl.multiple_of((t * 4 + to) * n, 16), n)
        if kind == 0:
            right = jnp.concatenate([gph[core], gpart[...]], axis=0)
        else:
            right = jnp.concatenate([cots[core], cotr[...]], axis=0)
        return dot(jnp.concatenate([mine[rows, :], theirs[rows, :]], axis=1), right, (1, 0))

    def hop(kind, t, n):
        send, relay, back = fsend[kind], frelay[kind], fback[kind]
        half = (slice(0, part[kind]), slice(part[kind], size[kind]))[n % 2]
        dst = relay.at[t, half] if n < 2 else back.at[t, n // 2 - 1, half]
        ahead = n in (0, 2, 3)
        to = ring[t] + (step if ahead else 4 - step)
        return remote(
            send.at[t, n // 2, half], dst, f_ss.at[kind], f_rs.at[kind, t, min(n // 2, 1)], dp, member(t, to)
        )

    def opposite(kind):
        for t in range(2):
            fsend[kind][t, 0] = block(kind, t, (ring[t] + 2) % 4).astype(BF16)
            hop(kind, t, 0).start()
            hop(kind, t, 1).start()

    def near(kind):
        for t in range(2):
            fsend[kind][t, 1] = block(kind, t, (ring[t] + step) % 4).astype(BF16)
            fsend[kind][t, 2] = block(kind, t, (ring[t] + 4 - step) % 4).astype(BF16)

    def near_push(kind):
        for t in range(2):
            hop(kind, t, 3).start()
            hop(kind, t, 4).start()

    def stay(kind):
        for t in range(2):
            own[kind][t] = block(kind, t, ring[t])

    def relays(kind):
        send, relay, cut = fsend[kind], frelay[kind], part[kind]
        for t in range(2):
            pltpu.make_async_copy(relay.at[t], relay.at[t], f_rs.at[kind, t, 0]).wait()
            for n, half in ((0, slice(0, cut)), (1, slice(cut, size[kind]))):
                send[t, 1 + n, half] = (
                    send[t, 1 + n, half].astype(F32) + relay[t, half].astype(F32)
                ).astype(BF16)
                hop(kind, t, 2 + 3 * n).start()

    def arrived(kind):
        for t in range(2):
            back = fback[kind].at[t]
            pltpu.make_async_copy(back, back, f_rs.at[kind, t, 1]).wait()
            own[kind][t] += fback[kind][t, 0].astype(F32) + fback[kind][t, 1].astype(F32)

    def cross():
        for t in range(2):
            here = ring[1 - t]
            for p in range(4):
                hsend[t, p] = jnp.concatenate(
                    [own0[t, 36 * p : 36 * p + 36], own1[t, 12 * p : 12 * p + 12]], axis=0
                ).astype(BF16)
            for k in (2, 1, 3):
                to = (here + k) % 4
                remote(
                    hsend.at[t, to], hrecv.at[t, here], h_ss.at[t], h_rs.at[t], dp, member(1 - t, to)
                ).start()
            pltpu.make_async_copy(hsend.at[t, here], hrecv.at[t, here], h_rs.at[t]).start()

    def z_target(n):
        return 4 * core + n // 2, (n % 2) * PLANE + xy

    def crossed():
        for t in range(2):
            pltpu.make_async_copy(hsend.at[t], hrecv.at[t], h_rs.at[t]).wait()
            total = hrecv[t, 0].astype(F32)
            for p in range(1, 4):
                total = total + hrecv[t, p].astype(F32)
            for j in range(4):
                zsend[2 * j + t] = total[:, 216 * j : 216 * j + 216].astype(BF16)

        @pl.loop(0, 8)
        def _(n):
            to_dp, to_seq = z_target(n)
            is_me = (to_dp == dp) & (to_seq == seq)

            @pl.when(is_me)
            def _():
                pltpu.make_async_copy(zsend.at[n], zrecv.at[zed], z_rs.at[0]).start()

            @pl.when(jnp.logical_not(is_me))
            def _():
                remote(zsend.at[n], zrecv.at[zed], z_ss.at[0], z_rs.at[0], to_dp, to_seq).start()

    def gathered():
        pltpu.make_async_copy(zsend, zrecv, z_rs.at[0]).wait()
        total = zrecv[0].astype(F32)
        for n in range(1, 8):
            total = total + zrecv[n].astype(F32)
        return total * FACTOR

    def z_sent(count):
        many = pl.ds(0, count)
        remote(
            zsend.at[many], zrecv.at[many], z_ss.at[0], z_rs.at[0], mate, seq
        ).wait_send()

    def all_sent():
        for kind in range(2):
            whole = fsend[kind]
            remote(whole, whole, f_ss.at[kind], f_rs.at[kind, 0, 0], mate, seq).wait_send()
        for t in range(2):
            many = pl.ds(0, 3)
            remote(
                hsend.at[t, many], hrecv.at[t, many], h_ss.at[t], h_rs.at[t], dp, member(1 - t, ring[1 - t] + 1)
            ).wait_send()
        pl.when(z_hi // 2 == core)(lambda: z_sent(7))
        pl.when(z_hi // 2 != core)(lambda: z_sent(8))

    opposite(0)
    take_all(ats, atr, 2)
    unpack(atr, slim)
    ttr[...] = slim[...].T
    tarr[...] = jnp.zeros((384, 3 * ROWS), F32)
    for p in range(2 * PLANE):
        if p < PLANE:
            begin = 48 * (p % 4) + 12 * (p // 4)
        else:
            begin = 12 * p
        tarr[begin : begin + 12, 0:ROWS] = ttr[18 * p : 18 * p + 12, :]
        rest = ttr[18 * p + 12 : 18 * p + 18, :]
        tarr[begin : begin + 6, ROWS : 2 * ROWS] = rest
        tarr[begin + 6 : begin + 12, 2 * ROWS :] = rest
    tmine[...] = tarr[...].astype(BF16)
    swap_t = remote(tmine, tpart, c_ss.at[3], c_rs.at[3], mate, seq)
    swap_t.start()
    near(0)
    near_push(0)
    swap_cot.wait_recv()
    swap_t.wait_recv()
    opposite(1)
    near(1)
    relays(0)
    near_push(1)
    stay(0)
    relays(1)
    stay(1)
    ordered = dot(move, slim[...].astype(BF16), (0, 0)).astype(BF16)
    branch = dot(ordered, wout[...], (1, 0))
    result[...] = (tok[...].astype(F32) + branch).astype(BF16)
    store_result = pltpu.make_async_copy(result, result_hbm, wsem.at[4])
    store_result.start()
    sent_all(xs, xr, 0)
    sent_all(gs, gr, 1)
    sent_all(ats, atr, 2)
    swap_cot.wait_send()
    swap_a.wait_send()
    swap_g.wait_send()
    swap_t.wait_send()
    arrived(0)
    arrived(1)
    cross()
    crossed()
    @pl.loop(1, PLANE)
    def _(k):
        push_rows(z_lo * PLANE + (xy + k) % PLANE)

    pltpu.make_async_copy(gbs.at[seq], gbr.at[seq], a_rs.at[3]).start()
    take_all(gbs, gbr, 3)
    unpack(gbr, wide)
    ordered = dot(move, wide[...].astype(BF16), (0, 0))
    gtok[...] = (cot[...].astype(F32) + ordered).astype(BF16)
    store_gtok = pltpu.make_async_copy(gtok, gtok_hbm, wsem.at[5])
    store_gtok.start()
    sent_all(gbs, gbr, 3)
    owned = gathered()
    gwq[...] = owned[:36, :]
    gwo[0:12, :] = owned[36:48, 0:144]
    gwo[12:18, :] = jnp.concatenate([owned[36:42, 144:216], owned[42:48, 144:216]], axis=1)
    all_sent()
    store_result.wait()
    store_gtok.wait()


def hand_over(*refs):
    for n in range(4):
        refs[4 + n][...] = refs[n][...]


def shards(tokens, cotangent, w_qkv, w_out):
    shape = tokens.shape
    vmem = pl.BlockSpec(memory_space=pltpu.VMEM)
    hbm = pl.BlockSpec(memory_space=pl.ANY)
    dma = pltpu.SemaphoreType.DMA
    scratch = [
        ((ROWS, D), BF16), ((ROWS, D), BF16), ((3 * HD, D), BF16), ((HD, D), BF16),
        ((ROWS, D), BF16), ((ROWS, D), BF16),
        ((ROWS, D), F32), ((ROWS, HD), F32), ((ROWS, D), F32), ((ROWS, D), BF16),
        ((SEQ, 4, D), BF16), ((SEQ, 4, D), BF16), ((SEQ, 4, HD), BF16), ((SEQ, 4, HD), BF16),
        ((SEQ, 4, HD), BF16), ((SEQ, 4, HD), BF16), ((SEQ, 4, D), BF16), ((SEQ, 4, D), BF16),
        ((2, 3 * ROWS, 864), BF16), ((3 * ROWS, 864), BF16),
        ((D, ROWS), F32), ((D, ROWS), F32), ((D, ROWS), BF16), ((D, ROWS), BF16),
        ((2, ROWS, 864), BF16), ((ROWS, 864), BF16), ((HD, ROWS), F32), ((384, 3 * ROWS), F32), ((384, 3 * ROWS), BF16), ((384, 3 * ROWS), BF16),
        ((HEADS * ROWS, HD), BF16), ((HEADS * ROWS, HD), BF16),
        ((HEADS * ROWS, HD), BF16), ((HEADS * ROWS, HD), BF16),
        ((HEADS * ROWS, ROWS), F32), ((HEADS * ROWS, ROWS), BF16),
        ((2, 3, 144, 864), BF16), ((2, 144, 864), BF16), ((2, 2, 144, 864), BF16), ((2, 144, 864), F32),
        ((2, 3, 48, 864), BF16), ((2, 48, 864), BF16), ((2, 2, 48, 864), BF16), ((2, 48, 864), F32),
        ((2, 4, 48, 864), BF16), ((2, 4, 48, 864), BF16), ((8, 48, 216), BF16), ((8, 48, 216), BF16),
    ]
    sems = [(6,), (4,), (4,), (4,), (4,), (2,), (2, 2, 2), (2,), (2,), (1,), (1,)]
    out_shape = (
        jax.ShapeDtypeStruct((ROWS, D), BF16),
        jax.ShapeDtypeStruct((ROWS, D), BF16),
        jax.ShapeDtypeStruct((36, 216), F32),
        jax.ShapeDtypeStruct((18, 144), F32),
    )
    outs = pl.pallas_call(
        kernel,
        out_shape=out_shape,
        in_specs=[hbm] * 4,
        out_specs=(hbm, hbm, vmem, vmem),
        scratch_shapes=[pltpu.VMEM(s, t) for s, t in scratch] + [dma(n) for n in sems],
        compiler_params=pltpu.CompilerParams(
            collective_id=0, has_side_effects=True, vmem_limit_bytes=56 * 1024 * 1024
        ),
    )(tokens.reshape(ROWS, D), cotangent.reshape(ROWS, D), w_qkv.T, w_out)
    result, gtok, gwq, gwo = pl.pallas_call(
        hand_over,
        out_shape=out_shape,
        in_specs=[vmem] * 4,
        out_specs=(vmem,) * 4,
    )(*outs)
    return (result.reshape(shape), gtok.reshape(shape), gwq, gwo)


def solution(mesh):
    in_specs = (P("dp", "seq", None, None), P("dp", "seq", None, None), P(), P())
    out_specs = (
        P("dp", "seq", None, None),
        P("dp", "seq", None, None),
        P("seq", "dp"),
        P("seq", "dp"),
    )
    return jax.shard_map(shards, mesh=mesh, in_specs=in_specs, out_specs=out_specs, check_vma=False)
```

```python
import functools

import jax
import jax.numpy as jnp
from jax import lax
from jax.experimental import pallas as pl
from jax.experimental.pallas import tpu as pltpu
from jax.sharding import PartitionSpec as P

MESH = pl.DeviceIdType.MESH
F32, BF16 = jnp.float32, jnp.bfloat16

D = 1152
HEADS = 8
HS = 72
HD = 576
ROWS = 128
SEQ = 32
PLANE = 16
EPS = 1e-6
SCALE = HS ** (-0.5)
FACTOR = 32768 ** (-0.5)


def dot(a, b, contract):
    return lax.dot_general(a, b, ((contract[:1], contract[1:]), ((), ())), preferred_element_type=F32)


def kernel(
    tok_hbm, cot_hbm, wqkv_hbm, wout_hbm,
    result_hbm, gtok_hbm, gwq, gwo,
    tok, cot, wqkv, wout, result, gtok,
    wide, slim, xhat, cotp,
    xs, xr, gs, gr, ats, atr, gbs, gbr,
    cots, cotr, ntr, arr, amine, apart, gph, gpart, ttr, tarr, tmine, tpart,
    qb, kb, vb, gab, probs, plow,
    fsend0, frelay0, fback0, own0, fsend1, frelay1, fback1, own1, hsend, hrecv, zsend, zrecv,
    wsem, a_ss, a_rs, c_ss, c_rs, f_ss, f_rs, h_ss, h_rs, z_ss, z_rs,
):
    dp, seq = lax.axis_index("dp"), lax.axis_index("seq")
    core, z_hi = dp % 2, dp // 2
    xy, z_lo = seq % PLANE, seq // PLANE
    mate = z_hi * 2 + 1 - core
    zed = z_hi * 2 + z_lo
    x, y = xy % 4, xy // 4
    step = 1 + 2 * core

    def remote(src, dst, send_sem, recv_sem, to_dp, to_seq):
        return pltpu.make_async_remote_copy(
            src_ref=src, dst_ref=dst, send_sem=send_sem, recv_sem=recv_sem,
            device_id=(to_dp, to_seq), device_id_type=MESH,
        )

    barrier = pltpu.get_barrier_semaphore()

    def greet(to_dp, to_seq):
        pl.semaphore_signal(barrier, inc=1, device_id=(to_dp, to_seq), device_id_type=MESH)

    @pl.loop(1, SEQ)
    def _(k):
        greet(dp, (seq + k) % SEQ)

    @pl.loop(1, 8)
    def _(k):
        greet((dp + k) % 8, xy)
        greet((dp + k) % 8, PLANE + xy)

    load_wqkv = pltpu.make_async_copy(wqkv_hbm, wqkv, wsem.at[0])
    load_wout = pltpu.make_async_copy(wout_hbm, wout, wsem.at[1])
    load_tok = pltpu.make_async_copy(tok_hbm, tok, wsem.at[2])
    load_cot = pltpu.make_async_copy(cot_hbm, cot, wsem.at[3])
    load_tok.start()
    load_cot.start()
    load_wout.start()
    load_wqkv.start()

    new = lax.broadcasted_iota(jnp.int32, (ROWS, ROWS), 0)
    old = lax.broadcasted_iota(jnp.int32, (ROWS, ROWS), 1)
    place = ((new >> 1) & 1) * 64 + (new >> 2) * 2 + (new & 1)
    move = jnp.where(place == old, 1.0, 0.0).astype(BF16)

    def pack(rows, block):
        for p in range(SEQ):
            block[p] = rows[4 * p : 4 * p + 4, :].astype(BF16)

    def unpack(block, rows):
        for p in range(SEQ):
            rows[4 * p : 4 * p + 4, :] = block[p].astype(F32)

    def push_all(src, dst, e):
        @pl.loop(1, SEQ)
        def _(k):
            to = (seq + k) % SEQ
            remote(src.at[to], dst.at[seq], a_ss.at[e], a_rs.at[e], dp, to).start()

        pltpu.make_async_copy(src.at[seq], dst.at[seq], a_rs.at[e]).start()

    def take_all(src, dst, e):
        pltpu.make_async_copy(src, dst, a_rs.at[e]).wait()

    def sent_all(src, dst, e):
        many = pl.ds(0, SEQ - 1)
        remote(src.at[many], dst.at[many], a_ss.at[e], a_rs.at[e], dp, (seq + 1) % SEQ).wait_send()

    load_tok.wait()
    wide[...] = dot(move, tok[...], (1, 0))
    pack(wide, xs)
    pl.semaphore_wait(barrier, SEQ - 1 + 14)
    push_all(xs, xr, 0)

    load_cot.wait()
    cotp[...] = dot(move, cot[...], (1, 0)).astype(BF16)
    load_wout.wait()
    slim[...] = dot(cotp[...], wout[...], (1, 1))
    pack(slim, gs)
    push_all(gs, gr, 1)
    for c in range(2):
        half = cotp[:, HD * c : HD * c + HD].astype(F32)
        gap0, gap1 = jnp.zeros((ROWS, 72), F32), jnp.zeros((ROWS, 144), F32)
        whole, left, right = [], [], []
        for j in range(4):
            b = 144 * j
            whole += [half[:, b : b + 144], gap0]
            left += [gap1, half[:, b : b + 72]]
            right += [gap1, half[:, b + 72 : b + 144]]
        for n, parts in enumerate((whole, left, right)):
            cots[c, n * ROWS : (n + 1) * ROWS, :] = jnp.concatenate(parts, axis=1).astype(BF16)
    swap_cot = remote(cots.at[1 - core], cotr, c_ss.at[0], c_rs.at[0], mate, seq)
    swap_cot.start()

    take_all(xs, xr, 0)
    unpack(xr, wide)
    moved = wide[...]
    centered = moved - jnp.mean(moved, axis=-1, keepdims=True)
    inv_std = lax.rsqrt(jnp.mean(centered * centered, axis=-1, keepdims=True) + EPS)
    x_hat = centered * inv_std
    xhat[...] = x_hat
    load_wqkv.wait()
    normed = x_hat.astype(BF16)
    query = dot(normed, wqkv[0:HD, :], (1, 1)).astype(BF16)
    key = dot(normed, wqkv[HD : 2 * HD, :], (1, 1)).astype(BF16)
    value = dot(normed, wqkv[2 * HD : 3 * HD, :], (1, 1)).astype(BF16)
    ntr[...] = xhat[...].T
    for p in range(PLANE):
        begin = 144 * (p % 4) + 36 * (p // 4)
        arr[begin : begin + 36, :] = ntr[36 * p : 36 * p + 36, :]
    arr[576:, :] = ntr[576:, :]
    amine[...] = arr[...].astype(BF16)
    swap_a = remote(amine, apart, c_ss.at[1], c_rs.at[1], mate, seq)
    swap_a.start()

    lane = lax.broadcasted_iota(jnp.int32, (ROWS, HD), 1)

    def stack(block, out):
        wide_block = block.astype(F32)
        for h in range(HEADS):
            inside = (lane >= h * HS) & (lane < (h + 1) * HS)
            out[h * ROWS : (h + 1) * ROWS, :] = jnp.where(inside, wide_block, 0.0).astype(BF16)

    def side(block):
        return jnp.concatenate([block[h * ROWS : (h + 1) * ROWS, :] for h in range(HEADS)], axis=1)

    stack(query, qb)
    stack(key, kb)
    stack(value, vb)
    scores = dot(qb[...], key, (1, 1)) * SCALE
    here = lax.broadcasted_iota(jnp.int32, (HEADS * ROWS, ROWS), 0)
    there = lax.broadcasted_iota(jnp.int32, (HEADS * ROWS, ROWS), 1)
    scores = jnp.where(((here ^ there) & 1) == 0, scores, -jnp.inf)
    expo = jnp.exp(scores - jnp.max(scores, axis=-1, keepdims=True))
    prob = expo / jnp.sum(expo, axis=-1, keepdims=True)
    probs[...] = prob
    plow[...] = prob.astype(BF16)
    slim[...] = dot(side(plow), vb[...], (1, 0))
    pack(slim, ats)
    push_all(ats, atr, 2)

    take_all(gs, gr, 1)
    unpack(gr, slim)
    stack(slim[...], gab)
    grad_probs = dot(gab[...], value, (1, 1))
    prob = probs[...]
    delta = jnp.sum(prob * grad_probs, axis=-1, keepdims=True)
    grad_scores = (prob * (grad_probs - delta) * SCALE).astype(BF16)
    grad_query = dot(side(grad_scores), kb[...], (1, 0))
    grad_key = dot(grad_scores, qb[...], (0, 0))
    grad_value = dot(plow[...], gab[...], (0, 0))
    grad_proj = jnp.concatenate([grad_query, grad_key, grad_value], axis=1)
    gph[0] = grad_proj[:, :864].astype(BF16)
    gph[1] = grad_proj[:, 864:].astype(BF16)
    swap_g = remote(gph.at[1 - core], gpart, c_ss.at[2], c_rs.at[2], mate, seq)
    swap_g.start()
    grad_proj = grad_proj.astype(BF16)

    grad_normed = dot(grad_proj, wqkv[...], (1, 0))
    x_hat = xhat[...]
    first = jnp.mean(grad_normed, axis=-1, keepdims=True)
    second = jnp.mean(grad_normed * x_hat, axis=-1, keepdims=True)
    wide[...] = (grad_normed - first - x_hat * second) * inv_std
    pack(wide, gbs)

    def push_rows(to):
        remote(gbs.at[to], gbr.at[seq], a_ss.at[3], a_rs.at[3], dp, to).start()

    @pl.loop(0, PLANE)
    def _(k):
        push_rows((1 - z_lo) * PLANE + (xy + k) % PLANE)

    swap_a.wait_recv()
    swap_g.wait_recv()

    size, part, piece = (144, 48), (80, 32), (36, 12)
    fsend, frelay, fback, own = (fsend0, fsend1), (frelay0, frelay1), (fback0, fback1), (own0, own1)
    ring = (x, y)

    def member(t, r):
        r = r % 4
        return z_lo * PLANE + (4 * y + r if t == 0 else 4 * r + x)

    def block(kind, t, to):
        mine, theirs = ((amine, apart), (tmine, tpart))[kind]
        n = size[kind]
        rows = pl.ds(pl.multiple_of((t * 4 + to) * n, 16), n)
        if kind == 0:
            right = jnp.concatenate([gph[core], gpart[...]], axis=0)
        else:
            right = jnp.concatenate([cots[core], cotr[...]], axis=0)
        return dot(jnp.concatenate([mine[rows, :], theirs[rows, :]], axis=1), right, (1, 0))

    def hop(kind, t, n):
        send, relay, back = fsend[kind], frelay[kind], fback[kind]
        half = (slice(0, part[kind]), slice(part[kind], size[kind]))[n % 2]
        dst = relay.at[t, half] if n < 2 else back.at[t, n // 2 - 1, half]
        ahead = n in (0, 2, 3)
        to = ring[t] + (step if ahead else 4 - step)
        return remote(
            send.at[t, n // 2, half], dst, f_ss.at[kind], f_rs.at[kind, t, min(n // 2, 1)], dp, member(t, to)
        )

    def opposite(kind):
        for t in range(2):
            fsend[kind][t, 0] = block(kind, t, (ring[t] + 2) % 4).astype(BF16)
            hop(kind, t, 0).start()
            hop(kind, t, 1).start()

    def near(kind):
        for t in range(2):
            fsend[kind][t, 1] = block(kind, t, (ring[t] + step) % 4).astype(BF16)
            fsend[kind][t, 2] = block(kind, t, (ring[t] + 4 - step) % 4).astype(BF16)

    def near_push(kind):
        for t in range(2):
            hop(kind, t, 3).start()
            hop(kind, t, 4).start()

    def stay(kind):
        for t in range(2):
            own[kind][t] = block(kind, t, ring[t])

    def relays(kind):
        send, relay, cut = fsend[kind], frelay[kind], part[kind]
        for t in range(2):
            pltpu.make_async_copy(relay.at[t], relay.at[t], f_rs.at[kind, t, 0]).wait()
            for n, half in ((0, slice(0, cut)), (1, slice(cut, size[kind]))):
                send[t, 1 + n, half] = (
                    send[t, 1 + n, half].astype(F32) + relay[t, half].astype(F32)
                ).astype(BF16)
                hop(kind, t, 2 + 3 * n).start()

    def arrived(kind):
        for t in range(2):
            back = fback[kind].at[t]
            pltpu.make_async_copy(back, back, f_rs.at[kind, t, 1]).wait()
            own[kind][t] += fback[kind][t, 0].astype(F32) + fback[kind][t, 1].astype(F32)

    def cross():
        for t in range(2):
            here = ring[1 - t]
            for p in range(4):
                hsend[t, p] = jnp.concatenate(
                    [own0[t, 36 * p : 36 * p + 36], own1[t, 12 * p : 12 * p + 12]], axis=0
                ).astype(BF16)
            for k in (2, 1, 3):
                to = (here + k) % 4
                remote(
                    hsend.at[t, to], hrecv.at[t, here], h_ss.at[t], h_rs.at[t], dp, member(1 - t, to)
                ).start()
            pltpu.make_async_copy(hsend.at[t, here], hrecv.at[t, here], h_rs.at[t]).start()

    def z_target(n):
        return 4 * core + n // 2, (n % 2) * PLANE + xy

    def crossed():
        for t in range(2):
            pltpu.make_async_copy(hsend.at[t], hrecv.at[t], h_rs.at[t]).wait()
            total = hrecv[t, 0].astype(F32)
            for p in range(1, 4):
                total = total + hrecv[t, p].astype(F32)
            for j in range(4):
                zsend[2 * j + t] = total[:, 216 * j : 216 * j + 216].astype(BF16)

        @pl.loop(0, 8)
        def _(n):
            to_dp, to_seq = z_target(n)
            is_me = (to_dp == dp) & (to_seq == seq)

            @pl.when(is_me)
            def _():
                pltpu.make_async_copy(zsend.at[n], zrecv.at[zed], z_rs.at[0]).start()

            @pl.when(jnp.logical_not(is_me))
            def _():
                remote(zsend.at[n], zrecv.at[zed], z_ss.at[0], z_rs.at[0], to_dp, to_seq).start()

    def gathered():
        pltpu.make_async_copy(zsend, zrecv, z_rs.at[0]).wait()
        total = zrecv[0].astype(F32)
        for n in range(1, 8):
            total = total + zrecv[n].astype(F32)
        return total * FACTOR

    def z_sent(count):
        many = pl.ds(0, count)
        remote(
            zsend.at[many], zrecv.at[many], z_ss.at[0], z_rs.at[0], mate, seq
        ).wait_send()

    def all_sent():
        for kind in range(2):
            whole = fsend[kind]
            remote(whole, whole, f_ss.at[kind], f_rs.at[kind, 0, 0], mate, seq).wait_send()
        for t in range(2):
            many = pl.ds(0, 3)
            remote(
                hsend.at[t, many], hrecv.at[t, many], h_ss.at[t], h_rs.at[t], dp, member(1 - t, ring[1 - t] + 1)
            ).wait_send()
        pl.when(z_hi // 2 == core)(lambda: z_sent(7))
        pl.when(z_hi // 2 != core)(lambda: z_sent(8))

    opposite(0)
    take_all(ats, atr, 2)
    unpack(atr, slim)
    ttr[...] = slim[...].T
    tarr[...] = jnp.zeros((384, 3 * ROWS), F32)
    for p in range(2 * PLANE):
        if p < PLANE:
            begin = 48 * (p % 4) + 12 * (p // 4)
        else:
            begin = 12 * p
        tarr[begin : begin + 12, 0:ROWS] = ttr[18 * p : 18 * p + 12, :]
        rest = ttr[18 * p + 12 : 18 * p + 18, :]
        tarr[begin : begin + 6, ROWS : 2 * ROWS] = rest
        tarr[begin + 6 : begin + 12, 2 * ROWS :] = rest
    tmine[...] = tarr[...].astype(BF16)
    swap_t = remote(tmine, tpart, c_ss.at[3], c_rs.at[3], mate, seq)
    swap_t.start()
    near(0)
    near_push(0)
    swap_cot.wait_recv()
    swap_t.wait_recv()
    opposite(1)
    near(1)
    relays(0)
    near_push(1)
    stay(0)
    relays(1)
    stay(1)
    ordered = dot(move, slim[...].astype(BF16), (0, 0)).astype(BF16)
    branch = dot(ordered, wout[...], (1, 0))
    result[...] = (tok[...].astype(F32) + branch).astype(BF16)
    store_result = pltpu.make_async_copy(result, result_hbm, wsem.at[4])
    store_result.start()
    sent_all(xs, xr, 0)
    sent_all(gs, gr, 1)
    sent_all(ats, atr, 2)
    swap_cot.wait_send()
    swap_a.wait_send()
    swap_g.wait_send()
    swap_t.wait_send()
    arrived(0)
    arrived(1)
    cross()
    crossed()
    @pl.loop(1, PLANE)
    def _(k):
        push_rows(z_lo * PLANE + (xy + k) % PLANE)

    pltpu.make_async_copy(gbs.at[seq], gbr.at[seq], a_rs.at[3]).start()
    take_all(gbs, gbr, 3)
    unpack(gbr, wide)
    ordered = dot(move, wide[...].astype(BF16), (0, 0))
    gtok[...] = (cot[...].astype(F32) + ordered).astype(BF16)
    store_gtok = pltpu.make_async_copy(gtok, gtok_hbm, wsem.at[5])
    store_gtok.start()
    sent_all(gbs, gbr, 3)
    owned = gathered()
    gwq[...] = owned[:36, :]
    gwo[0:12, :] = owned[36:48, 0:144]
    gwo[12:18, :] = jnp.concatenate([owned[36:42, 144:216], owned[42:48, 144:216]], axis=1)
    all_sent()
    store_result.wait()
    store_gtok.wait()


def hand_over(*refs):
    for n in range(4):
        refs[4 + n][...] = refs[n][...]


def shards(tokens, cotangent, w_qkv, w_out):
    shape = tokens.shape
    vmem = pl.BlockSpec(memory_space=pltpu.VMEM)
    hbm = pl.BlockSpec(memory_space=pl.ANY)
    dma = pltpu.SemaphoreType.DMA
    scratch = [
        ((ROWS, D), BF16), ((ROWS, D), BF16), ((3 * HD, D), BF16), ((HD, D), BF16),
        ((ROWS, D), BF16), ((ROWS, D), BF16),
        ((ROWS, D), F32), ((ROWS, HD), F32), ((ROWS, D), F32), ((ROWS, D), BF16),
        ((SEQ, 4, D), BF16), ((SEQ, 4, D), BF16), ((SEQ, 4, HD), BF16), ((SEQ, 4, HD), BF16),
        ((SEQ, 4, HD), BF16), ((SEQ, 4, HD), BF16), ((SEQ, 4, D), BF16), ((SEQ, 4, D), BF16),
        ((2, 3 * ROWS, 864), BF16), ((3 * ROWS, 864), BF16),
        ((D, ROWS), F32), ((D, ROWS), F32), ((D, ROWS), BF16), ((D, ROWS), BF16),
        ((2, ROWS, 864), BF16), ((ROWS, 864), BF16), ((HD, ROWS), F32), ((384, 3 * ROWS), F32), ((384, 3 * ROWS), BF16), ((384, 3 * ROWS), BF16),
        ((HEADS * ROWS, HD), BF16), ((HEADS * ROWS, HD), BF16),
        ((HEADS * ROWS, HD), BF16), ((HEADS * ROWS, HD), BF16),
        ((HEADS * ROWS, ROWS), F32), ((HEADS * ROWS, ROWS), BF16),
        ((2, 3, 144, 864), BF16), ((2, 144, 864), BF16), ((2, 2, 144, 864), BF16), ((2, 144, 864), F32),
        ((2, 3, 48, 864), BF16), ((2, 48, 864), BF16), ((2, 2, 48, 864), BF16), ((2, 48, 864), F32),
        ((2, 4, 48, 864), BF16), ((2, 4, 48, 864), BF16), ((8, 48, 216), BF16), ((8, 48, 216), BF16),
    ]
    sems = [(6,), (4,), (4,), (4,), (4,), (2,), (2, 2, 2), (2,), (2,), (1,), (1,)]
    out_shape = (
        jax.ShapeDtypeStruct((ROWS, D), BF16),
        jax.ShapeDtypeStruct((ROWS, D), BF16),
        jax.ShapeDtypeStruct((36, 216), F32),
        jax.ShapeDtypeStruct((18, 144), F32),
    )
    outs = pl.pallas_call(
        kernel,
        out_shape=out_shape,
        in_specs=[hbm] * 4,
        out_specs=(hbm, hbm, vmem, vmem),
        scratch_shapes=[pltpu.VMEM(s, t) for s, t in scratch] + [dma(n) for n in sems],
        compiler_params=pltpu.CompilerParams(
            collective_id=0, has_side_effects=True, vmem_limit_bytes=56 * 1024 * 1024
        ),
    )(tokens.reshape(ROWS, D), cotangent.reshape(ROWS, D), w_qkv.T, w_out)
    result, gtok, gwq, gwo = pl.pallas_call(
        hand_over,
        out_shape=out_shape,
        in_specs=[vmem] * 4,
        out_specs=(vmem,) * 4,
    )(*outs)
    return (result.reshape(shape), gtok.reshape(shape), gwq, gwo)


def solution(mesh):
    in_specs = (P("dp", "seq", None, None), P("dp", "seq", None, None), P(), P())
    out_specs = (
        P("dp", "seq", None, None),
        P("dp", "seq", None, None),
        P("seq", "dp"),
        P("seq", "dp"),
    )
    return jax.shard_map(shards, mesh=mesh, in_specs=in_specs, out_specs=out_specs, check_vma=False)
```

```python
import functools

import jax
import jax.numpy as jnp
from jax import lax
from jax.experimental import pallas as pl
from jax.experimental.pallas import tpu as pltpu
from jax.sharding import PartitionSpec as P

MESH = pl.DeviceIdType.MESH
F32, BF16 = jnp.float32, jnp.bfloat16

D = 1152
HEADS = 8
HS = 72
HD = 576
ROWS = 128
SEQ = 32
PLANE = 16
EPS = 1e-6
SCALE = HS ** (-0.5)
FACTOR = 32768 ** (-0.5)


def dot(a, b, contract):
    return lax.dot_general(a, b, ((contract[:1], contract[1:]), ((), ())), preferred_element_type=F32)


def kernel(
    tok_hbm, cot_hbm, wqkv_hbm, wout_hbm,
    result_hbm, gtok_hbm, zrecv,
    tok, cot, wqkv, wout, result, gtok,
    wide, slim, xhat, cotp,
    xs, xr, gs, gr, ats, atr, gbs, gbr,
    cots, cotr, ntr, arr, amine, apart, gph, gpart, ttr, tarr, tmine, tpart,
    qb, kb, vb, gab, probs, plow,
    fsend0, frelay0, fback0, own0, fsend1, frelay1, fback1, own1, hsend, hrecv, zsend,
    wsem, a_ss, a_rs, c_ss, c_rs, f_ss, f_rs, h_ss, h_rs, z_ss, z_rs,
):
    dp, seq = lax.axis_index("dp"), lax.axis_index("seq")
    core, z_hi = dp % 2, dp // 2
    xy, z_lo = seq % PLANE, seq // PLANE
    mate = z_hi * 2 + 1 - core
    zed = z_hi * 2 + z_lo
    x, y = xy % 4, xy // 4
    step = 1 + 2 * core

    def remote(src, dst, send_sem, recv_sem, to_dp, to_seq):
        return pltpu.make_async_remote_copy(
            src_ref=src, dst_ref=dst, send_sem=send_sem, recv_sem=recv_sem,
            device_id=(to_dp, to_seq), device_id_type=MESH,
        )

    barrier = pltpu.get_barrier_semaphore()

    def greet(to_dp, to_seq):
        pl.semaphore_signal(barrier, inc=1, device_id=(to_dp, to_seq), device_id_type=MESH)

    @pl.loop(1, SEQ)
    def _(k):
        greet(dp, (seq + k) % SEQ)

    @pl.loop(1, 8)
    def _(k):
        greet((dp + k) % 8, xy)
        greet((dp + k) % 8, PLANE + xy)

    load_wqkv = pltpu.make_async_copy(wqkv_hbm, wqkv, wsem.at[0])
    load_wout = pltpu.make_async_copy(wout_hbm, wout, wsem.at[1])
    load_tok = pltpu.make_async_copy(tok_hbm, tok, wsem.at[2])
    load_cot = pltpu.make_async_copy(cot_hbm, cot, wsem.at[3])
    load_tok.start()
    load_cot.start()
    load_wout.start()
    load_wqkv.start()

    new = lax.broadcasted_iota(jnp.int32, (ROWS, ROWS), 0)
    old = lax.broadcasted_iota(jnp.int32, (ROWS, ROWS), 1)
    place = ((new >> 1) & 1) * 64 + (new >> 2) * 2 + (new & 1)
    move = jnp.where(place == old, 1.0, 0.0).astype(BF16)

    def pack(rows, block):
        for p in range(SEQ):
            block[p] = rows[4 * p : 4 * p + 4, :].astype(BF16)

    def unpack(block, rows):
        for p in range(SEQ):
            rows[4 * p : 4 * p + 4, :] = block[p].astype(F32)

    def push_all(src, dst, e):
        @pl.loop(1, SEQ)
        def _(k):
            to = (seq + k) % SEQ
            remote(src.at[to], dst.at[seq], a_ss.at[e], a_rs.at[e], dp, to).start()

        pltpu.make_async_copy(src.at[seq], dst.at[seq], a_rs.at[e]).start()

    def take_all(src, dst, e):
        pltpu.make_async_copy(src, dst, a_rs.at[e]).wait()

    def sent_all(src, dst, e):
        many = pl.ds(0, SEQ - 1)
        remote(src.at[many], dst.at[many], a_ss.at[e], a_rs.at[e], dp, (seq + 1) % SEQ).wait_send()

    load_tok.wait()
    wide[...] = dot(move, tok[...], (1, 0))
    pack(wide, xs)
    pl.semaphore_wait(barrier, SEQ - 1 + 14)
    push_all(xs, xr, 0)

    load_cot.wait()
    cotp[...] = dot(move, cot[...], (1, 0)).astype(BF16)
    load_wout.wait()
    slim[...] = dot(cotp[...], wout[...], (1, 1))
    pack(slim, gs)
    push_all(gs, gr, 1)
    for c in range(2):
        half = cotp[:, HD * c : HD * c + HD].astype(F32)
        gap0, gap1 = jnp.zeros((ROWS, 72), F32), jnp.zeros((ROWS, 144), F32)
        whole, left, right = [], [], []
        for j in range(4):
            b = 144 * j
            whole += [half[:, b : b + 144], gap0]
            left += [gap1, half[:, b : b + 72]]
            right += [gap1, half[:, b + 72 : b + 144]]
        for n, parts in enumerate((whole, left, right)):
            cots[c, n * ROWS : (n + 1) * ROWS, :] = jnp.concatenate(parts, axis=1).astype(BF16)
    swap_cot = remote(cots.at[1 - core], cotr, c_ss.at[0], c_rs.at[0], mate, seq)
    swap_cot.start()

    take_all(xs, xr, 0)
    unpack(xr, wide)
    moved = wide[...]
    centered = moved - jnp.mean(moved, axis=-1, keepdims=True)
    inv_std = lax.rsqrt(jnp.mean(centered * centered, axis=-1, keepdims=True) + EPS)
    x_hat = centered * inv_std
    xhat[...] = x_hat
    load_wqkv.wait()
    normed = x_hat.astype(BF16)
    query = dot(normed, wqkv[0:HD, :], (1, 1)).astype(BF16)
    key = dot(normed, wqkv[HD : 2 * HD, :], (1, 1)).astype(BF16)
    value = dot(normed, wqkv[2 * HD : 3 * HD, :], (1, 1)).astype(BF16)
    ntr[...] = xhat[...].T
    for p in range(PLANE):
        begin = 144 * (p % 4) + 36 * (p // 4)
        arr[begin : begin + 36, :] = ntr[36 * p : 36 * p + 36, :]
    arr[576:, :] = ntr[576:, :]
    amine[...] = arr[...].astype(BF16)
    swap_a = remote(amine, apart, c_ss.at[1], c_rs.at[1], mate, seq)
    swap_a.start()

    lane = lax.broadcasted_iota(jnp.int32, (ROWS, HD), 1)

    def stack(block, out):
        wide_block = block.astype(F32)
        for h in range(HEADS):
            inside = (lane >= h * HS) & (lane < (h + 1) * HS)
            out[h * ROWS : (h + 1) * ROWS, :] = jnp.where(inside, wide_block, 0.0).astype(BF16)

    def side(block):
        return jnp.concatenate([block[h * ROWS : (h + 1) * ROWS, :] for h in range(HEADS)], axis=1)

    stack(query, qb)
    stack(key, kb)
    stack(value, vb)
    scores = dot(qb[...], key, (1, 1)) * SCALE
    here = lax.broadcasted_iota(jnp.int32, (HEADS * ROWS, ROWS), 0)
    there = lax.broadcasted_iota(jnp.int32, (HEADS * ROWS, ROWS), 1)
    scores = jnp.where(((here ^ there) & 1) == 0, scores, -jnp.inf)
    expo = jnp.exp(scores - jnp.max(scores, axis=-1, keepdims=True))
    prob = expo / jnp.sum(expo, axis=-1, keepdims=True)
    probs[...] = prob
    plow[...] = prob.astype(BF16)
    slim[...] = dot(side(plow), vb[...], (1, 0))
    pack(slim, ats)
    push_all(ats, atr, 2)

    take_all(gs, gr, 1)
    unpack(gr, slim)
    stack(slim[...], gab)
    grad_probs = dot(gab[...], value, (1, 1))
    prob = probs[...]
    delta = jnp.sum(prob * grad_probs, axis=-1, keepdims=True)
    grad_scores = (prob * (grad_probs - delta) * SCALE).astype(BF16)
    grad_query = dot(side(grad_scores), kb[...], (1, 0))
    grad_key = dot(grad_scores, qb[...], (0, 0))
    grad_value = dot(plow[...], gab[...], (0, 0))
    grad_proj = jnp.concatenate([g.astype(BF16) for g in (grad_query, grad_key, grad_value)], axis=1)
    gph[0] = grad_proj[:, :864]
    gph[1] = grad_proj[:, 864:]
    swap_g = remote(gph.at[1 - core], gpart, c_ss.at[2], c_rs.at[2], mate, seq)
    swap_g.start()

    grad_normed = dot(grad_proj, wqkv[...], (1, 0))
    x_hat = xhat[...]
    first = jnp.mean(grad_normed, axis=-1, keepdims=True)
    second = jnp.mean(grad_normed * x_hat, axis=-1, keepdims=True)
    wide[...] = (grad_normed - first - x_hat * second) * inv_std
    pack(wide, gbs)

    def push_rows(to):
        remote(gbs.at[to], gbr.at[seq], a_ss.at[3], a_rs.at[3], dp, to).start()

    @pl.loop(0, PLANE)
    def _(k):
        push_rows((1 - z_lo) * PLANE + (xy + k) % PLANE)

    swap_a.wait_recv()
    swap_g.wait_recv()

    size, part, piece = (144, 48), (80, 32), (36, 12)
    fsend, frelay, fback, own = (fsend0, fsend1), (frelay0, frelay1), (fback0, fback1), (own0, own1)
    ring = (x, y)

    def member(t, r):
        r = r % 4
        return z_lo * PLANE + (4 * y + r if t == 0 else 4 * r + x)

    def block(kind, t, to):
        mine, theirs = ((amine, apart), (tmine, tpart))[kind]
        n = size[kind]
        rows = pl.ds(pl.multiple_of((t * 4 + to) * n, 16), n)
        if kind == 0:
            right = jnp.concatenate([gph[core], gpart[...]], axis=0)
        else:
            right = jnp.concatenate([cots[core], cotr[...]], axis=0)
        return dot(jnp.concatenate([mine[rows, :], theirs[rows, :]], axis=1), right, (1, 0))

    def hop(kind, t, n):
        send, relay, back = fsend[kind], frelay[kind], fback[kind]
        half = (slice(0, part[kind]), slice(part[kind], size[kind]))[n % 2]
        dst = relay.at[t, half] if n < 2 else back.at[t, n // 2 - 1, half]
        ahead = n in (0, 2, 3)
        to = ring[t] + (step if ahead else 4 - step)
        return remote(
            send.at[t, n // 2, half], dst, f_ss.at[kind], f_rs.at[kind, t, min(n // 2, 1)], dp, member(t, to)
        )

    def opposite(kind):
        for t in range(2):
            fsend[kind][t, 0] = block(kind, t, (ring[t] + 2) % 4).astype(BF16)
            hop(kind, t, 0).start()
            hop(kind, t, 1).start()

    def near(kind):
        for t in range(2):
            fsend[kind][t, 1] = block(kind, t, (ring[t] + step) % 4).astype(BF16)
            fsend[kind][t, 2] = block(kind, t, (ring[t] + 4 - step) % 4).astype(BF16)

    def near_push(kind):
        for t in range(2):
            hop(kind, t, 3).start()
            hop(kind, t, 4).start()

    def stay(kind):
        for t in range(2):
            own[kind][t] = block(kind, t, ring[t])

    def relays(kind):
        send, relay, cut = fsend[kind], frelay[kind], part[kind]
        for t in range(2):
            pltpu.make_async_copy(relay.at[t], relay.at[t], f_rs.at[kind, t, 0]).wait()
            for n, half in ((0, slice(0, cut)), (1, slice(cut, size[kind]))):
                send[t, 1 + n, half] = (
                    send[t, 1 + n, half].astype(F32) + relay[t, half].astype(F32)
                ).astype(BF16)
                hop(kind, t, 2 + 3 * n).start()

    def arrived(kind):
        for t in range(2):
            back = fback[kind].at[t]
            pltpu.make_async_copy(back, back, f_rs.at[kind, t, 1]).wait()
            own[kind][t] += fback[kind][t, 0].astype(F32) + fback[kind][t, 1].astype(F32)

    def cross():
        for t in range(2):
            here = ring[1 - t]
            for p in range(4):
                hsend[t, p] = jnp.concatenate(
                    [own0[t, 36 * p : 36 * p + 36], own1[t, 12 * p : 12 * p + 12]], axis=0
                ).astype(BF16)
            for k in (2, 1, 3):
                to = (here + k) % 4
                remote(
                    hsend.at[t, to], hrecv.at[t, here], h_ss.at[t], h_rs.at[t], dp, member(1 - t, to)
                ).start()
            pltpu.make_async_copy(hsend.at[t, here], hrecv.at[t, here], h_rs.at[t]).start()

    def z_target(n):
        return 4 * core + n // 2, (n % 2) * PLANE + xy

    def crossed():
        for t in range(2):
            pltpu.make_async_copy(hsend.at[t], hrecv.at[t], h_rs.at[t]).wait()
            total = hrecv[t, 0].astype(F32)
            for p in range(1, 4):
                total = total + hrecv[t, p].astype(F32)
            for j in range(4):
                zsend[2 * j + t] = total[:, 216 * j : 216 * j + 216].astype(BF16)

        @pl.loop(0, 8)
        def _(n):
            to_dp, to_seq = z_target(n)
            is_me = (to_dp == dp) & (to_seq == seq)

            @pl.when(is_me)
            def _():
                pltpu.make_async_copy(zsend.at[n], zrecv.at[zed], z_rs.at[0]).start()

            @pl.when(jnp.logical_not(is_me))
            def _():
                remote(zsend.at[n], zrecv.at[zed], z_ss.at[0], z_rs.at[0], to_dp, to_seq).start()

    def gathered():
        pltpu.make_async_copy(zsend, zrecv, z_rs.at[0]).wait()

    def z_sent(count):
        many = pl.ds(0, count)
        remote(
            zsend.at[many], zrecv.at[many], z_ss.at[0], z_rs.at[0], mate, seq
        ).wait_send()

    def all_sent():
        for kind in range(2):
            whole = fsend[kind]
            remote(whole, whole, f_ss.at[kind], f_rs.at[kind, 0, 0], mate, seq).wait_send()
        for t in range(2):
            many = pl.ds(0, 3)
            remote(
                hsend.at[t, many], hrecv.at[t, many], h_ss.at[t], h_rs.at[t], dp, member(1 - t, ring[1 - t] + 1)
            ).wait_send()
        pl.when(z_hi // 2 == core)(lambda: z_sent(7))
        pl.when(z_hi // 2 != core)(lambda: z_sent(8))

    opposite(0)
    take_all(ats, atr, 2)
    unpack(atr, slim)
    ttr[...] = slim[...].T
    tarr[...] = jnp.zeros((384, 3 * ROWS), F32)
    for p in range(2 * PLANE):
        if p < PLANE:
            begin = 48 * (p % 4) + 12 * (p // 4)
        else:
            begin = 12 * p
        tarr[begin : begin + 12, 0:ROWS] = ttr[18 * p : 18 * p + 12, :]
        rest = ttr[18 * p + 12 : 18 * p + 18, :]
        tarr[begin : begin + 6, ROWS : 2 * ROWS] = rest
        tarr[begin + 6 : begin + 12, 2 * ROWS :] = rest
    tmine[...] = tarr[...].astype(BF16)
    swap_t = remote(tmine, tpart, c_ss.at[3], c_rs.at[3], mate, seq)
    swap_t.start()
    near(0)
    near_push(0)
    swap_cot.wait_recv()
    swap_t.wait_recv()
    opposite(1)
    near(1)
    relays(0)
    near_push(1)
    stay(0)
    relays(1)
    stay(1)
    ordered = dot(move, slim[...].astype(BF16), (0, 0)).astype(BF16)
    branch = dot(ordered, wout[...], (1, 0))
    result[...] = (tok[...].astype(F32) + branch).astype(BF16)
    store_result = pltpu.make_async_copy(result, result_hbm, wsem.at[4])
    store_result.start()
    sent_all(xs, xr, 0)
    sent_all(gs, gr, 1)
    sent_all(ats, atr, 2)
    swap_cot.wait_send()
    swap_a.wait_send()
    swap_g.wait_send()
    swap_t.wait_send()
    arrived(0)
    arrived(1)
    cross()
    crossed()
    @pl.loop(1, PLANE)
    def _(k):
        push_rows(z_lo * PLANE + (xy + k) % PLANE)

    pltpu.make_async_copy(gbs.at[seq], gbr.at[seq], a_rs.at[3]).start()
    take_all(gbs, gbr, 3)
    unpack(gbr, wide)
    ordered = dot(move, wide[...].astype(BF16), (0, 0))
    gtok[...] = (cot[...].astype(F32) + ordered).astype(BF16)
    store_gtok = pltpu.make_async_copy(gtok, gtok_hbm, wsem.at[5])
    store_gtok.start()
    sent_all(gbs, gbr, 3)
    gathered()
    all_sent()
    store_result.wait()
    store_gtok.wait()


def hand_over(result, gtok, pieces, result_out, gtok_out, gwq, gwo):
    result_out[...] = result[...]
    gtok_out[...] = gtok[...]
    total = pieces[0].astype(F32)
    for n in range(1, 8):
        total = total + pieces[n].astype(F32)
    owned = total * FACTOR
    gwq[...] = owned[:36, :]
    gwo[0:12, :] = owned[36:48, 0:144]
    gwo[12:18, :] = jnp.concatenate([owned[36:42, 144:216], owned[42:48, 144:216]], axis=1)


def shards(tokens, cotangent, w_qkv, w_out):
    shape = tokens.shape
    vmem = pl.BlockSpec(memory_space=pltpu.VMEM)
    hbm = pl.BlockSpec(memory_space=pl.ANY)
    dma = pltpu.SemaphoreType.DMA
    scratch = [
        ((ROWS, D), BF16), ((ROWS, D), BF16), ((3 * HD, D), BF16), ((HD, D), BF16),
        ((ROWS, D), BF16), ((ROWS, D), BF16),
        ((ROWS, D), F32), ((ROWS, HD), F32), ((ROWS, D), F32), ((ROWS, D), BF16),
        ((SEQ, 4, D), BF16), ((SEQ, 4, D), BF16), ((SEQ, 4, HD), BF16), ((SEQ, 4, HD), BF16),
        ((SEQ, 4, HD), BF16), ((SEQ, 4, HD), BF16), ((SEQ, 4, D), BF16), ((SEQ, 4, D), BF16),
        ((2, 3 * ROWS, 864), BF16), ((3 * ROWS, 864), BF16),
        ((D, ROWS), F32), ((D, ROWS), F32), ((D, ROWS), BF16), ((D, ROWS), BF16),
        ((2, ROWS, 864), BF16), ((ROWS, 864), BF16), ((HD, ROWS), F32), ((384, 3 * ROWS), F32), ((384, 3 * ROWS), BF16), ((384, 3 * ROWS), BF16),
        ((HEADS * ROWS, HD), BF16), ((HEADS * ROWS, HD), BF16),
        ((HEADS * ROWS, HD), BF16), ((HEADS * ROWS, HD), BF16),
        ((HEADS * ROWS, ROWS), F32), ((HEADS * ROWS, ROWS), BF16),
        ((2, 3, 144, 864), BF16), ((2, 144, 864), BF16), ((2, 2, 144, 864), BF16), ((2, 144, 864), F32),
        ((2, 3, 48, 864), BF16), ((2, 48, 864), BF16), ((2, 2, 48, 864), BF16), ((2, 48, 864), F32),
        ((2, 4, 48, 864), BF16), ((2, 4, 48, 864), BF16), ((8, 48, 216), BF16),
    ]
    sems = [(6,), (4,), (4,), (4,), (4,), (2,), (2, 2, 2), (2,), (2,), (1,), (1,)]
    out_shape = (
        jax.ShapeDtypeStruct((ROWS, D), BF16),
        jax.ShapeDtypeStruct((ROWS, D), BF16),
        jax.ShapeDtypeStruct((36, 216), F32),
        jax.ShapeDtypeStruct((18, 144), F32),
    )
    outs = pl.pallas_call(
        kernel,
        out_shape=out_shape[:2] + (jax.ShapeDtypeStruct((8, 48, 216), BF16),),
        in_specs=[hbm] * 4,
        out_specs=(hbm,) * 3,
        scratch_shapes=[pltpu.VMEM(s, t) for s, t in scratch] + [dma(n) for n in sems],
        compiler_params=pltpu.CompilerParams(
            collective_id=0, has_side_effects=True, vmem_limit_bytes=56 * 1024 * 1024
        ),
    )(tokens.reshape(ROWS, D), cotangent.reshape(ROWS, D), w_qkv.T, w_out)
    result, gtok, gwq, gwo = pl.pallas_call(
        hand_over,
        out_shape=out_shape,
        in_specs=[vmem] * 3,
        out_specs=(vmem,) * 4,
    )(*outs)
    return (result.reshape(shape), gtok.reshape(shape), gwq, gwo)


def solution(mesh):
    in_specs = (P("dp", "seq", None, None), P("dp", "seq", None, None), P(), P())
    out_specs = (
        P("dp", "seq", None, None),
        P("dp", "seq", None, None),
        P("seq", "dp"),
        P("seq", "dp"),
    )
    return jax.shard_map(shards, mesh=mesh, in_specs=in_specs, out_specs=out_specs, check_vma=False)
```

```python
import functools

import jax
import jax.numpy as jnp
from jax import lax
from jax.experimental import pallas as pl
from jax.experimental.pallas import tpu as pltpu
from jax.sharding import PartitionSpec as P

MESH = pl.DeviceIdType.MESH
F32, BF16 = jnp.float32, jnp.bfloat16

D = 1152
HEADS = 8
HS = 72
HD = 576
ROWS = 128
SEQ = 32
PLANE = 16
EPS = 1e-6
SCALE = HS ** (-0.5)
FACTOR = 32768 ** (-0.5)


def dot(a, b, contract):
    return lax.dot_general(a, b, ((contract[:1], contract[1:]), ((), ())), preferred_element_type=F32)


def kernel(
    tok_hbm, cot_hbm, wqkv_hbm, wout_hbm,
    result_hbm, gtok_hbm, zrecv,
    tok, cot, wqkv, wout, result, gtok,
    wide, slim, xhat, cotp,
    xs, xr, gs, gr, ats, atr, gbs, gbr,
    cots, cotr, ntr, arr, amine, apart, gph, gpart, ttr, tarr, tmine, tpart,
    qb, kb, vb, gab, probs, plow,
    fsend0, frelay0, fback0, own0, fsend1, frelay1, fback1, own1, hsend, hrecv, zsend,
    wsem, a_ss, a_rs, c_ss, c_rs, f_ss, f_rs, h_ss, h_rs, z_ss, z_rs,
):
    dp, seq = lax.axis_index("dp"), lax.axis_index("seq")
    core, z_hi = dp % 2, dp // 2
    xy, z_lo = seq % PLANE, seq // PLANE
    mate = z_hi * 2 + 1 - core
    zed = z_hi * 2 + z_lo
    x, y = xy % 4, xy // 4
    step = 1 + 2 * core

    def remote(src, dst, send_sem, recv_sem, to_dp, to_seq):
        return pltpu.make_async_remote_copy(
            src_ref=src, dst_ref=dst, send_sem=send_sem, recv_sem=recv_sem,
            device_id=(to_dp, to_seq), device_id_type=MESH,
        )

    barrier = pltpu.get_barrier_semaphore()

    def greet(to_dp, to_seq):
        pl.semaphore_signal(barrier, inc=1, device_id=(to_dp, to_seq), device_id_type=MESH)

    @pl.loop(1, SEQ)
    def _(k):
        greet(dp, (seq + k) % SEQ)

    @pl.loop(1, 8)
    def _(k):
        greet((dp + k) % 8, xy)
        greet((dp + k) % 8, PLANE + xy)

    load_wqkv = pltpu.make_async_copy(wqkv_hbm, wqkv, wsem.at[0])
    load_wout = pltpu.make_async_copy(wout_hbm, wout, wsem.at[1])
    load_tok = pltpu.make_async_copy(tok_hbm, tok, wsem.at[2])
    load_cot = pltpu.make_async_copy(cot_hbm, cot, wsem.at[3])
    load_tok.start()
    load_cot.start()
    load_wout.start()
    load_wqkv.start()

    new = lax.broadcasted_iota(jnp.int32, (ROWS, ROWS), 0)
    old = lax.broadcasted_iota(jnp.int32, (ROWS, ROWS), 1)
    place = ((new >> 1) & 1) * 64 + (new >> 2) * 2 + (new & 1)
    move = jnp.where(place == old, 1.0, 0.0).astype(BF16)

    def pack(rows, block):
        for p in range(SEQ):
            block[p] = rows[4 * p : 4 * p + 4, :].astype(BF16)

    def unpack(block, rows):
        for p in range(SEQ):
            rows[4 * p : 4 * p + 4, :] = block[p].astype(F32)

    def push_all(src, dst, e):
        @pl.loop(1, SEQ)
        def _(k):
            to = (seq + k) % SEQ
            remote(src.at[to], dst.at[seq], a_ss.at[e], a_rs.at[e], dp, to).start()

        pltpu.make_async_copy(src.at[seq], dst.at[seq], a_rs.at[e]).start()

    def take_all(src, dst, e):
        pltpu.make_async_copy(src, dst, a_rs.at[e]).wait()

    def sent_all(src, dst, e):
        many = pl.ds(0, SEQ - 1)
        remote(src.at[many], dst.at[many], a_ss.at[e], a_rs.at[e], dp, (seq + 1) % SEQ).wait_send()

    load_tok.wait()
    wide[...] = dot(move, tok[...], (1, 0))
    pack(wide, xs)
    pl.semaphore_wait(barrier, SEQ - 1 + 14)
    push_all(xs, xr, 0)

    load_cot.wait()
    cotp[...] = dot(move, cot[...], (1, 0)).astype(BF16)
    load_wout.wait()
    slim[...] = dot(cotp[...], wout[...], (1, 1))
    pack(slim, gs)
    push_all(gs, gr, 1)
    for c in range(2):
        half = cotp[:, HD * c : HD * c + HD].astype(F32)
        gap0, gap1 = jnp.zeros((ROWS, 72), F32), jnp.zeros((ROWS, 144), F32)
        whole, left, right = [], [], []
        for j in range(4):
            b = 144 * j
            whole += [half[:, b : b + 144], gap0]
            left += [gap1, half[:, b : b + 72]]
            right += [gap1, half[:, b + 72 : b + 144]]
        for n, parts in enumerate((whole, left, right)):
            cots[c, n * ROWS : (n + 1) * ROWS, :] = jnp.concatenate(parts, axis=1).astype(BF16)
    swap_cot = remote(cots.at[1 - core], cotr, c_ss.at[0], c_rs.at[0], mate, seq)
    swap_cot.start()

    take_all(xs, xr, 0)
    unpack(xr, wide)
    moved = wide[...]
    centered = moved - jnp.mean(moved, axis=-1, keepdims=True)
    inv_std = lax.rsqrt(jnp.mean(centered * centered, axis=-1, keepdims=True) + EPS)
    x_hat = centered * inv_std
    xhat[...] = x_hat
    load_wqkv.wait()
    normed = x_hat.astype(BF16)
    query = dot(normed, wqkv[0:HD, :], (1, 1)).astype(BF16)
    key = dot(normed, wqkv[HD : 2 * HD, :], (1, 1)).astype(BF16)
    value = dot(normed, wqkv[2 * HD : 3 * HD, :], (1, 1)).astype(BF16)
    ntr[...] = xhat[...].T
    for p in range(PLANE):
        begin = 144 * (p % 4) + 36 * (p // 4)
        arr[begin : begin + 36, :] = ntr[36 * p : 36 * p + 36, :]
    arr[576:, :] = ntr[576:, :]
    amine[...] = arr[...].astype(BF16)
    swap_a = remote(amine, apart, c_ss.at[1], c_rs.at[1], mate, seq)
    swap_a.start()

    lane = lax.broadcasted_iota(jnp.int32, (ROWS, HD), 1)

    def stack(block, out):
        wide_block = block.astype(F32)
        for h in range(HEADS):
            inside = (lane >= h * HS) & (lane < (h + 1) * HS)
            out[h * ROWS : (h + 1) * ROWS, :] = jnp.where(inside, wide_block, 0.0).astype(BF16)

    def side(block):
        return jnp.concatenate([block[h * ROWS : (h + 1) * ROWS, :] for h in range(HEADS)], axis=1)

    stack(query, qb)
    stack(key, kb)
    stack(value, vb)
    scores = dot(qb[...], key, (1, 1)) * SCALE
    here = lax.broadcasted_iota(jnp.int32, (HEADS * ROWS, ROWS), 0)
    there = lax.broadcasted_iota(jnp.int32, (HEADS * ROWS, ROWS), 1)
    scores = jnp.where(((here ^ there) & 1) == 0, scores, -jnp.inf)
    expo = jnp.exp(scores - jnp.max(scores, axis=-1, keepdims=True))
    prob = expo / jnp.sum(expo, axis=-1, keepdims=True)
    probs[...] = prob
    plow[...] = prob.astype(BF16)
    slim[...] = dot(side(plow), vb[...], (1, 0))
    pack(slim, ats)
    push_all(ats, atr, 2)

    take_all(gs, gr, 1)
    unpack(gr, slim)
    stack(slim[...], gab)
    grad_probs = dot(gab[...], value, (1, 1))
    prob = probs[...]
    delta = jnp.sum(prob * grad_probs, axis=-1, keepdims=True)
    grad_scores = (prob * (grad_probs - delta) * SCALE).astype(BF16)
    grad_query = dot(side(grad_scores), kb[...], (1, 0))
    grad_key = dot(grad_scores, qb[...], (0, 0))
    grad_value = dot(plow[...], gab[...], (0, 0))
    grad_proj = jnp.concatenate([g.astype(BF16) for g in (grad_query, grad_key, grad_value)], axis=1)
    gph[0] = grad_proj[:, :864]
    gph[1] = grad_proj[:, 864:]
    swap_g = remote(gph.at[1 - core], gpart, c_ss.at[2], c_rs.at[2], mate, seq)
    swap_g.start()

    grad_normed = dot(grad_proj, wqkv[...], (1, 0))
    x_hat = xhat[...]
    first = jnp.mean(grad_normed, axis=-1, keepdims=True)
    second = jnp.mean(grad_normed * x_hat, axis=-1, keepdims=True)
    wide[...] = (grad_normed - first - x_hat * second) * inv_std
    pack(wide, gbs)

    def push_rows(to):
        remote(gbs.at[to], gbr.at[seq], a_ss.at[3], a_rs.at[3], dp, to).start()

    swap_a.wait_recv()
    swap_g.wait_recv()

    size, part, piece = (144, 48), (80, 32), (36, 12)
    fsend, frelay, fback, own = (fsend0, fsend1), (frelay0, frelay1), (fback0, fback1), (own0, own1)
    ring = (x, y)

    def member(t, r):
        r = r % 4
        return z_lo * PLANE + (4 * y + r if t == 0 else 4 * r + x)

    def block(kind, t, to):
        mine, theirs = ((amine, apart), (tmine, tpart))[kind]
        n = size[kind]
        rows = pl.ds(pl.multiple_of((t * 4 + to) * n, 16), n)
        if kind == 0:
            right = jnp.concatenate([gph[core], gpart[...]], axis=0)
        else:
            right = jnp.concatenate([cots[core], cotr[...]], axis=0)
        return dot(jnp.concatenate([mine[rows, :], theirs[rows, :]], axis=1), right, (1, 0))

    def hop(kind, t, n):
        send, relay, back = fsend[kind], frelay[kind], fback[kind]
        half = (slice(0, part[kind]), slice(part[kind], size[kind]))[n % 2]
        dst = relay.at[t, half] if n < 2 else back.at[t, n // 2 - 1, half]
        ahead = n in (0, 2, 3)
        to = ring[t] + (step if ahead else 4 - step)
        return remote(
            send.at[t, n // 2, half], dst, f_ss.at[kind], f_rs.at[kind, t, min(n // 2, 1)], dp, member(t, to)
        )

    def opposite(kind):
        for t in range(2):
            fsend[kind][t, 0] = block(kind, t, (ring[t] + 2) % 4).astype(BF16)
            hop(kind, t, 0).start()
            hop(kind, t, 1).start()

    def near(kind):
        for t in range(2):
            fsend[kind][t, 1] = block(kind, t, (ring[t] + step) % 4).astype(BF16)
            fsend[kind][t, 2] = block(kind, t, (ring[t] + 4 - step) % 4).astype(BF16)

    def near_push(kind):
        for t in range(2):
            hop(kind, t, 3).start()
            hop(kind, t, 4).start()

    def stay(kind):
        for t in range(2):
            own[kind][t] = block(kind, t, ring[t])

    def relays(kind):
        send, relay, cut = fsend[kind], frelay[kind], part[kind]
        for t in range(2):
            pltpu.make_async_copy(relay.at[t], relay.at[t], f_rs.at[kind, t, 0]).wait()
            for n, half in ((0, slice(0, cut)), (1, slice(cut, size[kind]))):
                send[t, 1 + n, half] = (
                    send[t, 1 + n, half].astype(F32) + relay[t, half].astype(F32)
                ).astype(BF16)
                hop(kind, t, 2 + 3 * n).start()

    def arrived(kind):
        for t in range(2):
            back = fback[kind].at[t]
            pltpu.make_async_copy(back, back, f_rs.at[kind, t, 1]).wait()
            own[kind][t] += fback[kind][t, 0].astype(F32) + fback[kind][t, 1].astype(F32)

    def cross():
        for t in range(2):
            here = ring[1 - t]
            for p in range(4):
                hsend[t, p] = jnp.concatenate(
                    [own0[t, 36 * p : 36 * p + 36], own1[t, 12 * p : 12 * p + 12]], axis=0
                ).astype(BF16)
            for k in (2, 1, 3):
                to = (here + k) % 4
                remote(
                    hsend.at[t, to], hrecv.at[t, here], h_ss.at[t], h_rs.at[t], dp, member(1 - t, to)
                ).start()
            pltpu.make_async_copy(hsend.at[t, here], hrecv.at[t, here], h_rs.at[t]).start()

    def z_target(n):
        return 4 * core + n // 2, (n % 2) * PLANE + xy

    def crossed():
        for t in range(2):
            pltpu.make_async_copy(hsend.at[t], hrecv.at[t], h_rs.at[t]).wait()
            total = hrecv[t, 0].astype(F32)
            for p in range(1, 4):
                total = total + hrecv[t, p].astype(F32)
            for j in range(4):
                zsend[2 * j + t] = total[:, 216 * j : 216 * j + 216].astype(BF16)

        @pl.loop(0, 8)
        def _(n):
            to_dp, to_seq = z_target(n)
            is_me = (to_dp == dp) & (to_seq == seq)

            @pl.when(is_me)
            def _():
                pltpu.make_async_copy(zsend.at[n], zrecv.at[zed], z_rs.at[0]).start()

            @pl.when(jnp.logical_not(is_me))
            def _():
                remote(zsend.at[n], zrecv.at[zed], z_ss.at[0], z_rs.at[0], to_dp, to_seq).start()

    def gathered():
        pltpu.make_async_copy(zsend, zrecv, z_rs.at[0]).wait()

    def z_sent(count):
        many = pl.ds(0, count)
        remote(
            zsend.at[many], zrecv.at[many], z_ss.at[0], z_rs.at[0], mate, seq
        ).wait_send()

    def all_sent():
        for kind in range(2):
            whole = fsend[kind]
            remote(whole, whole, f_ss.at[kind], f_rs.at[kind, 0, 0], mate, seq).wait_send()
        for t in range(2):
            many = pl.ds(0, 3)
            remote(
                hsend.at[t, many], hrecv.at[t, many], h_ss.at[t], h_rs.at[t], dp, member(1 - t, ring[1 - t] + 1)
            ).wait_send()
        pl.when(z_hi // 2 == core)(lambda: z_sent(7))
        pl.when(z_hi // 2 != core)(lambda: z_sent(8))

    opposite(0)
    take_all(ats, atr, 2)
    unpack(atr, slim)
    ttr[...] = slim[...].T
    tarr[...] = jnp.zeros((384, 3 * ROWS), F32)
    for p in range(2 * PLANE):
        if p < PLANE:
            begin = 48 * (p % 4) + 12 * (p // 4)
        else:
            begin = 12 * p
        tarr[begin : begin + 12, 0:ROWS] = ttr[18 * p : 18 * p + 12, :]
        rest = ttr[18 * p + 12 : 18 * p + 18, :]
        tarr[begin : begin + 6, ROWS : 2 * ROWS] = rest
        tarr[begin + 6 : begin + 12, 2 * ROWS :] = rest
    tmine[...] = tarr[...].astype(BF16)
    swap_t = remote(tmine, tpart, c_ss.at[3], c_rs.at[3], mate, seq)
    swap_t.start()
    near(0)
    near_push(0)

    @pl.loop(0, PLANE)
    def _(k):
        push_rows((1 - z_lo) * PLANE + (xy + k) % PLANE)

    swap_cot.wait_recv()
    swap_t.wait_recv()
    opposite(1)
    near(1)
    relays(0)
    near_push(1)
    stay(0)
    relays(1)
    stay(1)
    ordered = dot(move, slim[...].astype(BF16), (0, 0)).astype(BF16)
    branch = dot(ordered, wout[...], (1, 0))
    result[...] = (tok[...].astype(F32) + branch).astype(BF16)
    store_result = pltpu.make_async_copy(result, result_hbm, wsem.at[4])
    store_result.start()
    sent_all(xs, xr, 0)
    sent_all(gs, gr, 1)
    sent_all(ats, atr, 2)
    swap_cot.wait_send()
    swap_a.wait_send()
    swap_g.wait_send()
    swap_t.wait_send()
    arrived(0)
    arrived(1)
    cross()
    crossed()
    @pl.loop(1, PLANE)
    def _(k):
        push_rows(z_lo * PLANE + (xy + k) % PLANE)

    pltpu.make_async_copy(gbs.at[seq], gbr.at[seq], a_rs.at[3]).start()
    take_all(gbs, gbr, 3)
    unpack(gbr, wide)
    ordered = dot(move, wide[...].astype(BF16), (0, 0))
    gtok[...] = (cot[...].astype(F32) + ordered).astype(BF16)
    store_gtok = pltpu.make_async_copy(gtok, gtok_hbm, wsem.at[5])
    store_gtok.start()
    sent_all(gbs, gbr, 3)
    gathered()
    all_sent()
    store_result.wait()
    store_gtok.wait()


def hand_over(result, gtok, pieces, result_out, gtok_out, gwq, gwo):
    result_out[...] = result[...]
    gtok_out[...] = gtok[...]
    total = pieces[0].astype(F32)
    for n in range(1, 8):
        total = total + pieces[n].astype(F32)
    owned = total * FACTOR
    gwq[...] = owned[:36, :]
    gwo[0:12, :] = owned[36:48, 0:144]
    gwo[12:18, :] = jnp.concatenate([owned[36:42, 144:216], owned[42:48, 144:216]], axis=1)


def shards(tokens, cotangent, w_qkv, w_out):
    shape = tokens.shape
    vmem = pl.BlockSpec(memory_space=pltpu.VMEM)
    hbm = pl.BlockSpec(memory_space=pl.ANY)
    dma = pltpu.SemaphoreType.DMA
    scratch = [
        ((ROWS, D), BF16), ((ROWS, D), BF16), ((3 * HD, D), BF16), ((HD, D), BF16),
        ((ROWS, D), BF16), ((ROWS, D), BF16),
        ((ROWS, D), F32), ((ROWS, HD), F32), ((ROWS, D), F32), ((ROWS, D), BF16),
        ((SEQ, 4, D), BF16), ((SEQ, 4, D), BF16), ((SEQ, 4, HD), BF16), ((SEQ, 4, HD), BF16),
        ((SEQ, 4, HD), BF16), ((SEQ, 4, HD), BF16), ((SEQ, 4, D), BF16), ((SEQ, 4, D), BF16),
        ((2, 3 * ROWS, 864), BF16), ((3 * ROWS, 864), BF16),
        ((D, ROWS), F32), ((D, ROWS), F32), ((D, ROWS), BF16), ((D, ROWS), BF16),
        ((2, ROWS, 864), BF16), ((ROWS, 864), BF16), ((HD, ROWS), F32), ((384, 3 * ROWS), F32), ((384, 3 * ROWS), BF16), ((384, 3 * ROWS), BF16),
        ((HEADS * ROWS, HD), BF16), ((HEADS * ROWS, HD), BF16),
        ((HEADS * ROWS, HD), BF16), ((HEADS * ROWS, HD), BF16),
        ((HEADS * ROWS, ROWS), F32), ((HEADS * ROWS, ROWS), BF16),
        ((2, 3, 144, 864), BF16), ((2, 144, 864), BF16), ((2, 2, 144, 864), BF16), ((2, 144, 864), F32),
        ((2, 3, 48, 864), BF16), ((2, 48, 864), BF16), ((2, 2, 48, 864), BF16), ((2, 48, 864), F32),
        ((2, 4, 48, 864), BF16), ((2, 4, 48, 864), BF16), ((8, 48, 216), BF16),
    ]
    sems = [(6,), (4,), (4,), (4,), (4,), (2,), (2, 2, 2), (2,), (2,), (1,), (1,)]
    out_shape = (
        jax.ShapeDtypeStruct((ROWS, D), BF16),
        jax.ShapeDtypeStruct((ROWS, D), BF16),
        jax.ShapeDtypeStruct((36, 216), F32),
        jax.ShapeDtypeStruct((18, 144), F32),
    )
    outs = pl.pallas_call(
        kernel,
        out_shape=out_shape[:2] + (jax.ShapeDtypeStruct((8, 48, 216), BF16),),
        in_specs=[hbm] * 4,
        out_specs=(hbm,) * 3,
        scratch_shapes=[pltpu.VMEM(s, t) for s, t in scratch] + [dma(n) for n in sems],
        compiler_params=pltpu.CompilerParams(
            collective_id=0, has_side_effects=True, vmem_limit_bytes=56 * 1024 * 1024
        ),
    )(tokens.reshape(ROWS, D), cotangent.reshape(ROWS, D), w_qkv.T, w_out)
    result, gtok, gwq, gwo = pl.pallas_call(
        hand_over,
        out_shape=out_shape,
        in_specs=[vmem] * 3,
        out_specs=(vmem,) * 4,
    )(*outs)
    return (result.reshape(shape), gtok.reshape(shape), gwq, gwo)


def solution(mesh):
    in_specs = (P("dp", "seq", None, None), P("dp", "seq", None, None), P(), P())
    out_specs = (
        P("dp", "seq", None, None),
        P("dp", "seq", None, None),
        P("seq", "dp"),
        P("seq", "dp"),
    )
    return jax.shard_map(shards, mesh=mesh, in_specs=in_specs, out_specs=out_specs, check_vma=False)
```

```python
import functools

import jax
import jax.numpy as jnp
from jax import lax
from jax.experimental import pallas as pl
from jax.experimental.pallas import tpu as pltpu
from jax.sharding import PartitionSpec as P

MESH = pl.DeviceIdType.MESH
F32, BF16 = jnp.float32, jnp.bfloat16

D = 1152
HEADS = 8
HS = 72
HD = 576
ROWS = 128
SEQ = 32
PLANE = 16
EPS = 1e-6
SCALE = HS ** (-0.5)
FACTOR = 32768 ** (-0.5)


def dot(a, b, contract):
    return lax.dot_general(a, b, ((contract[:1], contract[1:]), ((), ())), preferred_element_type=F32)


def kernel(
    tok_hbm, cot_hbm, wqkv_hbm, wout_hbm,
    result_hbm, gtok_hbm, zrecv,
    tok, cot, wqkv, wout, result, gtok,
    wide, slim, xhat, cotp,
    xs, xr, gs, gr, ats, atr, gbs, gbr,
    cots, cotr, ntr, arr, amine, apart, gph, gpart, ttr, tarr, tmine, tpart,
    qb, kb, vb, gab, probs, plow,
    fsend0, frelay0, fback0, own0, fsend1, frelay1, fback1, own1, hsend, hrecv, zsend,
    wsem, a_ss, a_rs, c_ss, c_rs, f_ss, f_rs, h_ss, h_rs, z_ss, z_rs,
):
    dp, seq = lax.axis_index("dp"), lax.axis_index("seq")
    core, z_hi = dp % 2, dp // 2
    xy, z_lo = seq % PLANE, seq // PLANE
    mate = z_hi * 2 + 1 - core
    zed = z_hi * 2 + z_lo
    x, y = xy % 4, xy // 4
    step = 1 + 2 * core

    def remote(src, dst, send_sem, recv_sem, to_dp, to_seq):
        return pltpu.make_async_remote_copy(
            src_ref=src, dst_ref=dst, send_sem=send_sem, recv_sem=recv_sem,
            device_id=(to_dp, to_seq), device_id_type=MESH,
        )

    barrier = pltpu.get_barrier_semaphore()

    def greet(to_dp, to_seq):
        pl.semaphore_signal(barrier, inc=1, device_id=(to_dp, to_seq), device_id_type=MESH)

    @pl.loop(1, SEQ)
    def _(k):
        greet(dp, (seq + k) % SEQ)

    @pl.loop(1, 8)
    def _(k):
        greet((dp + k) % 8, xy)
        greet((dp + k) % 8, PLANE + xy)

    load_wqkv = pltpu.make_async_copy(wqkv_hbm, wqkv, wsem.at[0])
    load_wout = pltpu.make_async_copy(wout_hbm, wout, wsem.at[1])
    load_tok = pltpu.make_async_copy(tok_hbm, tok, wsem.at[2])
    load_cot = pltpu.make_async_copy(cot_hbm, cot, wsem.at[3])
    load_tok.start()
    load_cot.start()
    load_wout.start()
    load_wqkv.start()

    new = lax.broadcasted_iota(jnp.int32, (ROWS, ROWS), 0)
    old = lax.broadcasted_iota(jnp.int32, (ROWS, ROWS), 1)
    place = ((new >> 1) & 1) * 64 + (new >> 2) * 2 + (new & 1)
    move = jnp.where(place == old, 1.0, 0.0).astype(BF16)

    def pack(rows, block):
        for p in range(SEQ):
            block[p] = rows[4 * p : 4 * p + 4, :].astype(BF16)

    def unpack(block, rows):
        for p in range(SEQ):
            rows[4 * p : 4 * p + 4, :] = block[p].astype(F32)

    def push_all(src, dst, e):
        @pl.loop(1, SEQ)
        def _(k):
            to = (seq + k) % SEQ
            remote(src.at[to], dst.at[seq], a_ss.at[e], a_rs.at[e], dp, to).start()

        pltpu.make_async_copy(src.at[seq], dst.at[seq], a_rs.at[e]).start()

    def take_all(src, dst, e):
        pltpu.make_async_copy(src, dst, a_rs.at[e]).wait()

    def sent_all(src, dst, e):
        many = pl.ds(0, SEQ - 1)
        remote(src.at[many], dst.at[many], a_ss.at[e], a_rs.at[e], dp, (seq + 1) % SEQ).wait_send()

    load_tok.wait()
    wide[...] = dot(move, tok[...], (1, 0))
    pack(wide, xs)
    pl.semaphore_wait(barrier, SEQ - 1 + 14)
    push_all(xs, xr, 0)

    load_cot.wait()
    cotp[...] = dot(move, cot[...], (1, 0)).astype(BF16)
    load_wout.wait()
    slim[...] = dot(cotp[...], wout[...], (1, 1))
    pack(slim, gs)
    push_all(gs, gr, 1)
    for c in range(2):
        half = cotp[:, HD * c : HD * c + HD].astype(F32)
        gap0, gap1 = jnp.zeros((ROWS, 72), F32), jnp.zeros((ROWS, 144), F32)
        whole, left, right = [], [], []
        for j in range(4):
            b = 144 * j
            whole += [half[:, b : b + 144], gap0]
            left += [gap1, half[:, b : b + 72]]
            right += [gap1, half[:, b + 72 : b + 144]]
        for n, parts in enumerate((whole, left, right)):
            cots[c, n * ROWS : (n + 1) * ROWS, :] = jnp.concatenate(parts, axis=1).astype(BF16)
    swap_cot = remote(cots.at[1 - core], cotr, c_ss.at[0], c_rs.at[0], mate, seq)
    swap_cot.start()

    take_all(xs, xr, 0)
    unpack(xr, wide)
    moved = wide[...]
    centered = moved - jnp.mean(moved, axis=-1, keepdims=True)
    inv_std = lax.rsqrt(jnp.mean(centered * centered, axis=-1, keepdims=True) + EPS)
    x_hat = centered * inv_std
    xhat[...] = x_hat
    load_wqkv.wait()
    normed = x_hat.astype(BF16)
    query = dot(normed, wqkv[0:HD, :], (1, 1)).astype(BF16)
    key = dot(normed, wqkv[HD : 2 * HD, :], (1, 1)).astype(BF16)
    value = dot(normed, wqkv[2 * HD : 3 * HD, :], (1, 1)).astype(BF16)
    ntr[...] = xhat[...].T
    for p in range(PLANE):
        begin = 144 * (p % 4) + 36 * (p // 4)
        arr[begin : begin + 36, :] = ntr[36 * p : 36 * p + 36, :]
    arr[576:, :] = ntr[576:, :]
    amine[...] = arr[...].astype(BF16)
    swap_a = remote(amine, apart, c_ss.at[1], c_rs.at[1], mate, seq)
    swap_a.start()

    lane = lax.broadcasted_iota(jnp.int32, (ROWS, HD), 1)

    def stack(block, out):
        wide_block = block.astype(F32)
        for h in range(HEADS):
            inside = (lane >= h * HS) & (lane < (h + 1) * HS)
            out[h * ROWS : (h + 1) * ROWS, :] = jnp.where(inside, wide_block, 0.0).astype(BF16)

    def side(block):
        return jnp.concatenate([block[h * ROWS : (h + 1) * ROWS, :] for h in range(HEADS)], axis=1)

    stack(query, qb)
    stack(key, kb)
    stack(value, vb)
    scores = dot(qb[...], key, (1, 1)) * SCALE
    here = lax.broadcasted_iota(jnp.int32, (HEADS * ROWS, ROWS), 0)
    there = lax.broadcasted_iota(jnp.int32, (HEADS * ROWS, ROWS), 1)
    scores = jnp.where(((here ^ there) & 1) == 0, scores, -jnp.inf)
    expo = jnp.exp(scores - jnp.max(scores, axis=-1, keepdims=True))
    prob = expo / jnp.sum(expo, axis=-1, keepdims=True)
    probs[...] = prob
    plow[...] = prob.astype(BF16)
    slim[...] = dot(side(plow), vb[...], (1, 0))
    pack(slim, ats)
    push_all(ats, atr, 2)

    take_all(gs, gr, 1)
    unpack(gr, slim)
    stack(slim[...], gab)
    grad_probs = dot(gab[...], value, (1, 1))
    prob = probs[...]
    delta = jnp.sum(prob * grad_probs, axis=-1, keepdims=True)
    grad_scores = (prob * (grad_probs - delta) * SCALE).astype(BF16)
    grad_query = dot(side(grad_scores), kb[...], (1, 0))
    grad_key = dot(grad_scores, qb[...], (0, 0))
    grad_value = dot(plow[...], gab[...], (0, 0))
    grad_proj = jnp.concatenate([g.astype(BF16) for g in (grad_query, grad_key, grad_value)], axis=1)
    gph[0] = grad_proj[:, :864]
    gph[1] = grad_proj[:, 864:]
    swap_g = remote(gph.at[1 - core], gpart, c_ss.at[2], c_rs.at[2], mate, seq)
    swap_g.start()

    grad_normed = dot(grad_proj, wqkv[...], (1, 0))
    x_hat = xhat[...]
    first = jnp.mean(grad_normed, axis=-1, keepdims=True)
    second = jnp.mean(grad_normed * x_hat, axis=-1, keepdims=True)
    wide[...] = (grad_normed - first - x_hat * second) * inv_std
    pack(wide, gbs)

    def push_rows(to):
        remote(gbs.at[to], gbr.at[seq], a_ss.at[3], a_rs.at[3], dp, to).start()

    @pl.loop(0, PLANE)
    def _(k):
        push_rows((1 - z_lo) * PLANE + (xy + k) % PLANE)

    swap_a.wait_recv()
    swap_g.wait_recv()

    size, part, piece = (144, 48), (80, 32), (36, 12)
    fsend, frelay, fback, own = (fsend0, fsend1), (frelay0, frelay1), (fback0, fback1), (own0, own1)
    ring = (x, y)

    def member(t, r):
        r = r % 4
        return z_lo * PLANE + (4 * y + r if t == 0 else 4 * r + x)

    def block(kind, t, to):
        mine, theirs = ((amine, apart), (tmine, tpart))[kind]
        n = size[kind]
        rows = pl.ds(pl.multiple_of((t * 4 + to) * n, 16), n)
        if kind == 0:
            right = jnp.concatenate([gph[core], gpart[...]], axis=0)
        else:
            right = jnp.concatenate([cots[core], cotr[...]], axis=0)
        return dot(jnp.concatenate([mine[rows, :], theirs[rows, :]], axis=1), right, (1, 0))

    def hop(kind, t, n):
        send, relay, back = fsend[kind], frelay[kind], fback[kind]
        half = (slice(0, part[kind]), slice(part[kind], size[kind]))[n % 2]
        dst = relay.at[t, half] if n < 2 else back.at[t, n // 2 - 1, half]
        ahead = n in (0, 2, 3)
        to = ring[t] + (step if ahead else 4 - step)
        return remote(
            send.at[t, n // 2, half], dst, f_ss.at[kind], f_rs.at[kind, t, min(n // 2, 1)], dp, member(t, to)
        )

    def opposite(kind):
        for t in range(2):
            fsend[kind][t, 0] = block(kind, t, (ring[t] + 2) % 4).astype(BF16)
            hop(kind, t, 0).start()
            hop(kind, t, 1).start()

    def near(kind):
        for t in range(2):
            fsend[kind][t, 1] = block(kind, t, (ring[t] + step) % 4).astype(BF16)
            fsend[kind][t, 2] = block(kind, t, (ring[t] + 4 - step) % 4).astype(BF16)

    def near_push(kind):
        for t in range(2):
            hop(kind, t, 3).start()
            hop(kind, t, 4).start()

    def stay(kind):
        for t in range(2):
            own[kind][t] = block(kind, t, ring[t])

    def relays(kind):
        send, relay, cut = fsend[kind], frelay[kind], part[kind]
        for t in range(2):
            pltpu.make_async_copy(relay.at[t], relay.at[t], f_rs.at[kind, t, 0]).wait()
            for n, half in ((0, slice(0, cut)), (1, slice(cut, size[kind]))):
                send[t, 1 + n, half] = (
                    send[t, 1 + n, half].astype(F32) + relay[t, half].astype(F32)
                ).astype(BF16)
                hop(kind, t, 2 + 3 * n).start()

    def arrived(kind):
        for t in range(2):
            back = fback[kind].at[t]
            pltpu.make_async_copy(back, back, f_rs.at[kind, t, 1]).wait()
            own[kind][t] += fback[kind][t, 0].astype(F32) + fback[kind][t, 1].astype(F32)

    def cross():
        for t in range(2):
            here = ring[1 - t]
            for p in range(4):
                hsend[t, p] = jnp.concatenate(
                    [own0[t, 36 * p : 36 * p + 36], own1[t, 12 * p : 12 * p + 12]], axis=0
                ).astype(BF16)
            for k in (2, 1, 3):
                to = (here + k) % 4
                remote(
                    hsend.at[t, to], hrecv.at[t, here], h_ss.at[t], h_rs.at[t], dp, member(1 - t, to)
                ).start()
            pltpu.make_async_copy(hsend.at[t, here], hrecv.at[t, here], h_rs.at[t]).start()

    def z_target(n):
        return 4 * core + n // 2, (n % 2) * PLANE + xy

    def crossed():
        for t in range(2):
            pltpu.make_async_copy(hsend.at[t], hrecv.at[t], h_rs.at[t]).wait()
            total = hrecv[t, 0].astype(F32)
            for p in range(1, 4):
                total = total + hrecv[t, p].astype(F32)
            for j in range(4):
                zsend[2 * j + t] = total[:, 216 * j : 216 * j + 216].astype(BF16)

            @pl.loop(0, 4)
            def _(j):
                n = 2 * j + t
                to_dp, to_seq = z_target(n)
                is_me = (to_dp == dp) & (to_seq == seq)

                @pl.when(is_me)
                def _():
                    pltpu.make_async_copy(zsend.at[n], zrecv.at[zed], z_rs.at[0]).start()

                @pl.when(jnp.logical_not(is_me))
                def _():
                    remote(zsend.at[n], zrecv.at[zed], z_ss.at[0], z_rs.at[0], to_dp, to_seq).start()

    def gathered():
        pltpu.make_async_copy(zsend, zrecv, z_rs.at[0]).wait()

    def z_sent(count):
        many = pl.ds(0, count)
        remote(
            zsend.at[many], zrecv.at[many], z_ss.at[0], z_rs.at[0], mate, seq
        ).wait_send()

    def all_sent():
        for kind in range(2):
            whole = fsend[kind]
            remote(whole, whole, f_ss.at[kind], f_rs.at[kind, 0, 0], mate, seq).wait_send()
        for t in range(2):
            many = pl.ds(0, 3)
            remote(
                hsend.at[t, many], hrecv.at[t, many], h_ss.at[t], h_rs.at[t], dp, member(1 - t, ring[1 - t] + 1)
            ).wait_send()
        pl.when(z_hi // 2 == core)(lambda: z_sent(7))
        pl.when(z_hi // 2 != core)(lambda: z_sent(8))

    opposite(0)
    take_all(ats, atr, 2)
    unpack(atr, slim)
    ttr[...] = slim[...].T
    tarr[...] = jnp.zeros((384, 3 * ROWS), F32)
    for p in range(2 * PLANE):
        if p < PLANE:
            begin = 48 * (p % 4) + 12 * (p // 4)
        else:
            begin = 12 * p
        tarr[begin : begin + 12, 0:ROWS] = ttr[18 * p : 18 * p + 12, :]
        rest = ttr[18 * p + 12 : 18 * p + 18, :]
        tarr[begin : begin + 6, ROWS : 2 * ROWS] = rest
        tarr[begin + 6 : begin + 12, 2 * ROWS :] = rest
    tmine[...] = tarr[...].astype(BF16)
    swap_t = remote(tmine, tpart, c_ss.at[3], c_rs.at[3], mate, seq)
    swap_t.start()
    near(0)
    near_push(0)
    swap_cot.wait_recv()
    swap_t.wait_recv()
    opposite(1)
    near(1)
    relays(0)
    near_push(1)
    stay(0)
    relays(1)
    stay(1)
    ordered = dot(move, slim[...].astype(BF16), (0, 0)).astype(BF16)
    branch = dot(ordered, wout[...], (1, 0))
    result[...] = (tok[...].astype(F32) + branch).astype(BF16)
    store_result = pltpu.make_async_copy(result, result_hbm, wsem.at[4])
    store_result.start()
    sent_all(xs, xr, 0)
    sent_all(gs, gr, 1)
    sent_all(ats, atr, 2)
    swap_cot.wait_send()
    swap_a.wait_send()
    swap_g.wait_send()
    swap_t.wait_send()
    arrived(0)
    arrived(1)
    cross()
    crossed()
    @pl.loop(1, PLANE)
    def _(k):
        push_rows(z_lo * PLANE + (xy + k) % PLANE)

    pltpu.make_async_copy(gbs.at[seq], gbr.at[seq], a_rs.at[3]).start()
    take_all(gbs, gbr, 3)
    unpack(gbr, wide)
    ordered = dot(move, wide[...].astype(BF16), (0, 0))
    gtok[...] = (cot[...].astype(F32) + ordered).astype(BF16)
    store_gtok = pltpu.make_async_copy(gtok, gtok_hbm, wsem.at[5])
    store_gtok.start()
    sent_all(gbs, gbr, 3)
    gathered()
    all_sent()
    store_result.wait()
    store_gtok.wait()


def hand_over(result, gtok, pieces, result_out, gtok_out, gwq, gwo):
    result_out[...] = result[...]
    gtok_out[...] = gtok[...]
    total = pieces[0].astype(F32)
    for n in range(1, 8):
        total = total + pieces[n].astype(F32)
    owned = total * FACTOR
    gwq[...] = owned[:36, :]
    gwo[0:12, :] = owned[36:48, 0:144]
    gwo[12:18, :] = jnp.concatenate([owned[36:42, 144:216], owned[42:48, 144:216]], axis=1)


def shards(tokens, cotangent, w_qkv, w_out):
    shape = tokens.shape
    vmem = pl.BlockSpec(memory_space=pltpu.VMEM)
    hbm = pl.BlockSpec(memory_space=pl.ANY)
    dma = pltpu.SemaphoreType.DMA
    scratch = [
        ((ROWS, D), BF16), ((ROWS, D), BF16), ((3 * HD, D), BF16), ((HD, D), BF16),
        ((ROWS, D), BF16), ((ROWS, D), BF16),
        ((ROWS, D), F32), ((ROWS, HD), F32), ((ROWS, D), F32), ((ROWS, D), BF16),
        ((SEQ, 4, D), BF16), ((SEQ, 4, D), BF16), ((SEQ, 4, HD), BF16), ((SEQ, 4, HD), BF16),
        ((SEQ, 4, HD), BF16), ((SEQ, 4, HD), BF16), ((SEQ, 4, D), BF16), ((SEQ, 4, D), BF16),
        ((2, 3 * ROWS, 864), BF16), ((3 * ROWS, 864), BF16),
        ((D, ROWS), F32), ((D, ROWS), F32), ((D, ROWS), BF16), ((D, ROWS), BF16),
        ((2, ROWS, 864), BF16), ((ROWS, 864), BF16), ((HD, ROWS), F32), ((384, 3 * ROWS), F32), ((384, 3 * ROWS), BF16), ((384, 3 * ROWS), BF16),
        ((HEADS * ROWS, HD), BF16), ((HEADS * ROWS, HD), BF16),
        ((HEADS * ROWS, HD), BF16), ((HEADS * ROWS, HD), BF16),
        ((HEADS * ROWS, ROWS), F32), ((HEADS * ROWS, ROWS), BF16),
        ((2, 3, 144, 864), BF16), ((2, 144, 864), BF16), ((2, 2, 144, 864), BF16), ((2, 144, 864), F32),
        ((2, 3, 48, 864), BF16), ((2, 48, 864), BF16), ((2, 2, 48, 864), BF16), ((2, 48, 864), F32),
        ((2, 4, 48, 864), BF16), ((2, 4, 48, 864), BF16), ((8, 48, 216), BF16),
    ]
    sems = [(6,), (4,), (4,), (4,), (4,), (2,), (2, 2, 2), (2,), (2,), (1,), (1,)]
    out_shape = (
        jax.ShapeDtypeStruct((ROWS, D), BF16),
        jax.ShapeDtypeStruct((ROWS, D), BF16),
        jax.ShapeDtypeStruct((36, 216), F32),
        jax.ShapeDtypeStruct((18, 144), F32),
    )
    outs = pl.pallas_call(
        kernel,
        out_shape=out_shape[:2] + (jax.ShapeDtypeStruct((8, 48, 216), BF16),),
        in_specs=[hbm] * 4,
        out_specs=(hbm,) * 3,
        scratch_shapes=[pltpu.VMEM(s, t) for s, t in scratch] + [dma(n) for n in sems],
        compiler_params=pltpu.CompilerParams(
            collective_id=0, has_side_effects=True, vmem_limit_bytes=56 * 1024 * 1024
        ),
    )(tokens.reshape(ROWS, D), cotangent.reshape(ROWS, D), w_qkv.T, w_out)
    result, gtok, gwq, gwo = pl.pallas_call(
        hand_over,
        out_shape=out_shape,
        in_specs=[vmem] * 3,
        out_specs=(vmem,) * 4,
    )(*outs)
    return (result.reshape(shape), gtok.reshape(shape), gwq, gwo)


def solution(mesh):
    in_specs = (P("dp", "seq", None, None), P("dp", "seq", None, None), P(), P())
    out_specs = (
        P("dp", "seq", None, None),
        P("dp", "seq", None, None),
        P("seq", "dp"),
        P("seq", "dp"),
    )
    return jax.shard_map(shards, mesh=mesh, in_specs=in_specs, out_specs=out_specs, check_vma=False)
```
